128 devices in a mesh: dp: 32 (over x, z_hi, y), seq: 4 (over z_lo, core).
Axes of the slice: x: 4, y: 4, z: 4 (z_hi: 2, z_lo: 2; z = z_hi * 2 + z_lo), core: 2. Of those that a mesh axis runs over, the one named last changes fastest.
Arguments:
- hidden: bfloat16 [32768, 5120], P(('dp', 'seq')), may hold values from -24 to 24
- query_base: bfloat16 [32768, 2560], P(('dp', 'seq')), may hold values from -6 to 6
- key_base: bfloat16 [32768, 2560], P(('dp', 'seq')), may hold values from -6 to 6
- value_base: bfloat16 [32768, 2560], P(('dp', 'seq')), may hold values from -6 to 6
- cotangent: bfloat16 [32768, 2560], P(('dp', 'seq')), may hold values from -0.375 to 0.375
- down_query: bfloat16 [5120, 128], replicated, may hold values from -0.078125 to 0.078125
- down_value: bfloat16 [5120, 128], replicated, may hold values from -0.078125 to 0.078125
- up_query: bfloat16 [128, 2560], replicated, may hold values from -0.5 to 0.5
- up_value: bfloat16 [128, 2560], replicated, may hold values from -0.5 to 0.5
- key_blocks: int32 [20, 8, 5], P('seq'), may hold values from 0 to 7, as said below
- block_counts: int32 [20, 8], P('seq'), may hold values from 1 to 5
Outputs:
- attended: bfloat16 [32768, 2560], P(('dp', 'seq'))
- grad_down: float32 [5120, 2, 128], P(('dp', 'seq'))
- grad_up: float32 [128, 2, 2560], P('dp', None, 'seq')
The draws below stay inside these ranges and needn't reach their ends.
Inputs may be any that keep to these rules, and one draw needn't show every extreme that they name: For head h and query block i the first block_counts[h, i] entries of key_blocks[h, i] are distinct key blocks in rising order; the later entries are valid block numbers and are not attended to.
All inputs are finite; a program needn't handle non-finite values.
Results may differ from the reference program's by a relative error of at most 0.033.
Values may be sent and summed in bfloat16 or wider, within the bound.
No kernel may reach another device: no remote copies, remote signals or barrier semaphores. Data moves between devices by JAX's collectives and lax.ppermute only.
A program may use at most 128 MiB of HBM per device.

```python
import math
import jax
import jax.numpy as jnp
from jax import lax

D = 5120
HEADS = 20
HD = 128
R = 128
HH = 2560
SEQ_LEN = 1024
NB = 8
KMAX = 5
TOKENS = 32768
N_DP = 32


def draw_query_base(key, part):
    key = jax.random.fold_in(key, 3)
    field = jnp.clip(jax.random.normal(key, (TOKENS, HH)), -6.0, 6.0)
    return field.astype(jnp.bfloat16)


def draw_key_base(key, part):
    key = jax.random.fold_in(key, 5)
    field = jnp.clip(jax.random.normal(key, (TOKENS, HH)), -6.0, 6.0)
    return field.astype(jnp.bfloat16)


def block_band(key):
    radius_key, stride_key, widest_key = jax.random.split(key, 3)
    radius = jax.random.randint(radius_key, (HEADS,), 0, KMAX // 2)
    stride = jax.random.randint(stride_key, (HEADS,), 2, 5)
    widest = jax.random.randint(widest_key, (), 0, HEADS)
    radius = jnp.where(jnp.arange(HEADS) == widest, NB, radius)
    row_index = jnp.arange(NB)[:, None]
    col_index = jnp.arange(NB)[None, :]
    distance = jnp.abs(row_index - col_index)[None, :, :]
    member = (distance <= radius[:, None, None]) | (col_index[None, :, :] == 0) | (distance % stride[:, None, None] == 0)
    priority = jnp.where(col_index[None, :, :] == 0, 0, 1 + distance * NB + col_index[None, :, :])
    ahead = jnp.sum((member[:, :, None, :] & (priority[:, :, None, :] < priority[:, :, :, None])).astype(jnp.int32), axis=-1)
    chosen = member & (ahead < KMAX)
    ranking = jnp.where(chosen, col_index[None, :, :], NB + col_index[None, :, :])
    listing = jnp.argsort(ranking, axis=-1, stable=True)[:, :, :KMAX].astype(jnp.int32)
    counts = jnp.sum(chosen.astype(jnp.int32), axis=-1).astype(jnp.int32)
    return (listing, counts)


def draw_key_blocks(key, part):
    return block_band(key)[0]


def draw_block_counts(key, part):
    return block_band(key)[1]


def strengthened(values, key, source, target, shards_of, factor):
    owner, partner = [(jnp.arange(values.shape[dim]) // (values.shape[dim] // shards_of)).reshape([-1 if axis == dim else 1 for axis in range(values.ndim)]) for dim in (source, target)]
    chosen = jax.random.permutation(key, shards_of)[partner]
    strong = (owner == chosen) | (owner == (partner + shards_of // 2) % shards_of)
    return jnp.where(strong, factor * values, values)


def block_scale(key, dims, cuts, smallest, largest):
    factor_of, own = 1.0, jax.random.fold_in(key, 6)
    for dim, blocks in cuts:
        draws = jnp.exp(jax.random.uniform(jax.random.fold_in(own, dim), (blocks,), jnp.float32, smallest / len(cuts), largest / len(cuts)))
        factor_of = factor_of * jnp.repeat(draws, dims[dim] // blocks).reshape([-1 if axis == dim else 1 for axis in range(len(dims))])
    return factor_of


def scatter_about(stream_key, extent, deviation, reach, shards=(), dtype=jnp.bfloat16):
    result = deviation * jax.random.normal(stream_key, extent, jnp.float32)
    if shards:
        result = result * block_scale(stream_key, extent, shards, -0.22, 0.18)
    return jnp.clip(result, -reach, reach).astype(dtype)


def noise_with(stream_key, shape, width, bound, cuts, heavy, kind=jnp.bfloat16):
    drawn = width * jax.random.normal(stream_key, shape, jnp.float32)
    if cuts:
        drawn = drawn * block_scale(stream_key, shape, cuts, -0.22, 0.18)
    return jnp.clip(strengthened(drawn, jax.random.fold_in(stream_key, 3), *heavy), -bound, bound).astype(kind)


def setup_inputs(seed: int = 0) -> dict:
    key_of = jax.random.split(jax.random.key(seed), 12)
    hidden = noise_with(key_of[0], (TOKENS, D), 1.0, 24.0, ((0, 128),), (0, 1, 128, 5.5))
    query_base = draw_query_base(jax.random.fold_in(key_of[11], 71), 0)
    key_base = draw_key_base(jax.random.fold_in(key_of[11], 71), 0)
    value_base = scatter_about(key_of[3], (TOKENS, HH), 1.0, 6.0, ((0, 128),))
    cotangent = scatter_about(key_of[4], (TOKENS, HH), 0.0625, 0.375, ((0, 128),))
    down_query = scatter_about(key_of[5], (D, R), D ** -0.5, 0.078125)
    down_value = scatter_about(key_of[6], (D, R), D ** -0.5, 0.078125)
    up_query = scatter_about(key_of[7], (R, HH), R ** -0.5, 0.5)
    up_value = scatter_about(key_of[8], (R, HH), R ** -0.5, 0.5)
    key_blocks = draw_key_blocks(jax.random.fold_in(key_of[11], 71), 0)
    block_counts = draw_block_counts(jax.random.fold_in(key_of[11], 71), 0)
    return dict(hidden=hidden, query_base=query_base, key_base=key_base, value_base=value_base, cotangent=cotangent, down_query=down_query, down_value=down_value, up_query=up_query, up_value=up_value, key_blocks=key_blocks, block_counts=block_counts)


def head_pass(queries, key_rows, values, upstream, blocks, counts):
    block_total, slot_count = blocks.shape
    head_width = queries.shape[1]
    length = queries.shape[0] // block_total
    score_scale = 1.0 / math.sqrt(head_width)
    highest = lax.Precision.HIGHEST
    query_tiles = queries.reshape(block_total, length, head_width).astype(jnp.float32)
    key_tiles = key_rows.reshape(block_total, length, head_width)[blocks].reshape(block_total, slot_count * length, head_width).astype(jnp.float32)
    value_tiles = values.reshape(block_total, length, head_width)[blocks].reshape(block_total, slot_count * length, head_width).astype(jnp.float32)
    upstream_tiles = upstream.reshape(block_total, length, head_width).astype(jnp.float32)
    listed = jnp.arange(slot_count)[None, :] < counts[:, None]
    spread_mask = jnp.repeat(listed, length, axis=1)
    scores = jnp.einsum('nqd,nkd->nqk', query_tiles, key_tiles, precision=highest) * score_scale
    scores = jnp.where(spread_mask[:, None, :], scores, -1e+30)
    row_max = lax.optimization_barrier(jnp.max(scores, axis=-1, keepdims=True))
    powers = jnp.exp(scores - row_max)
    probability = powers / lax.optimization_barrier(jnp.sum(powers, axis=-1, keepdims=True))
    weights = lax.optimization_barrier(probability.astype(jnp.bfloat16)).astype(jnp.float32)
    attended = jnp.einsum('nqk,nkd->nqd', weights, value_tiles, precision=highest).astype(jnp.bfloat16)
    grad_probs = jnp.einsum('nqd,nkd->nqk', upstream_tiles, value_tiles, precision=highest)
    centred = grad_probs - lax.optimization_barrier(jnp.sum(probability * grad_probs, axis=-1, keepdims=True))
    shifted = lax.optimization_barrier((probability * centred).astype(jnp.bfloat16)).astype(jnp.float32)
    grad_query = (jnp.einsum('nqk,nkd->nqd', shifted, key_tiles, precision=highest) * score_scale).astype(jnp.bfloat16)
    pieces = jnp.einsum('nqk,nqd->nkd', weights, upstream_tiles, precision=highest).reshape(block_total, slot_count, length, head_width)
    chooser = ((blocks[:, :, None] == jnp.arange(block_total)[None, None, :]) & listed[:, :, None]).astype(jnp.float32)
    grad_value = jnp.einsum('nsj,nsbd->jbd', chooser, pieces, precision=highest).astype(jnp.bfloat16)
    return (attended.reshape(-1, head_width), grad_query.reshape(-1, head_width), grad_value.reshape(-1, head_width))

def reference(hidden, query_base, key_base, value_base, cotangent, down_query, down_value, up_query, up_value, key_blocks, block_counts):
    low_query = jnp.dot(hidden, down_query, preferred_element_type=jnp.float32).astype(jnp.bfloat16)
    low_value = jnp.dot(hidden, down_value, preferred_element_type=jnp.float32).astype(jnp.bfloat16)
    queries = (query_base.astype(jnp.float32) + jnp.dot(low_query, up_query, preferred_element_type=jnp.float32)).astype(jnp.bfloat16)
    values = (value_base.astype(jnp.float32) + jnp.dot(low_value, up_value, preferred_element_type=jnp.float32)).astype(jnp.bfloat16)

    def to_heads(array):
        return array.reshape(N_DP, SEQ_LEN, HEADS, HD).transpose(0, 2, 1, 3).reshape(N_DP * HEADS, SEQ_LEN, HD)

    def from_heads(array):
        return array.reshape(N_DP, HEADS, SEQ_LEN, HD).transpose(0, 2, 1, 3).reshape(TOKENS, HEADS * HD)
    head_ids = jnp.tile(jnp.arange(HEADS), N_DP)

    def one_pass(items):
        head_queries, head_keys, head_values, head_upstream, head_index = items
        return head_pass(head_queries, head_keys, head_values, head_upstream, key_blocks[head_index], block_counts[head_index])
    results = lax.map(one_pass, (to_heads(queries), to_heads(key_base), to_heads(values), to_heads(cotangent), head_ids))
    attended = from_heads(results[0])
    grad_query = from_heads(results[1])
    grad_value = from_heads(results[2])
    grad_up = jnp.stack([jnp.dot(low_query.T, grad_query, preferred_element_type=jnp.float32), jnp.dot(low_value.T, grad_value, preferred_element_type=jnp.float32)], axis=1)
    low_grad_query = jnp.dot(grad_query, up_query.T, preferred_element_type=jnp.float32).astype(jnp.bfloat16)
    low_grad_value = jnp.dot(grad_value, up_value.T, preferred_element_type=jnp.float32).astype(jnp.bfloat16)
    grad_down = jnp.stack([jnp.dot(hidden.T, low_grad_query, preferred_element_type=jnp.float32), jnp.dot(hidden.T, low_grad_value, preferred_element_type=jnp.float32)], axis=1)
    return (attended, grad_down, grad_up)
```

```python
import functools
import math

import jax
import jax.numpy as jnp
from jax import lax
from jax.experimental import pallas as pl
from jax.experimental.pallas import tpu as pltpu
from jax.sharding import Mesh
from jax.sharding import PartitionSpec as P

HEADS = 20
HD = 128
R = 128
NB = 8
ROWS = 256
K_CHUNKS = ((0, 10), (10, 10))
V_CHUNKS = ((0, 5), (5, 5), (10, 5), (15, 5))
SCALE = 1.0 / math.sqrt(HD)
SCALE2 = SCALE * math.log2(math.e)
F32 = jnp.float32
BF16 = jnp.bfloat16


def nn(a, b):
    return lax.dot_general(a, b, (((1,), (0,)), ((), ())), preferred_element_type=F32)


def nt(a, b):
    return lax.dot_general(a, b, (((1,), (1,)), ((), ())), preferred_element_type=F32)


def tn(a, b):
    return lax.dot_general(a, b, (((0,), (0,)), ((), ())), preferred_element_type=F32)


def weight_kernel(
    h0, bias_ref, qb_ref, lowq_ref, upq_ref, cot_ref, upv_ref, k0, k1, k2, k3, wt_ref, g_ref, lgv_ref
):
    step = pl.program_id(0)
    query = (qb_ref[...].astype(F32) + nn(lowq_ref[...], upq_ref[...])).astype(BF16)
    g = nt(cot_ref[...], upv_ref[...]).astype(BF16)
    g_ref[...] = g
    first_half = lax.broadcasted_iota(jnp.int32, (1, ROWS), 1) < ROWS // 2
    parts = []
    for r, key_ref in enumerate((k0, k1, k2, k3)):
        s = nt(key_ref[...], query) * SCALE2
        for b in range(2):
            j = 2 * r + b
            bias = jnp.where(first_half, bias_ref[h0 + step, j], bias_ref[h0 + step, NB + j])
            parts.append(s[b * 128 : (b + 1) * 128] + bias)
    top = functools.reduce(jnp.maximum, [jnp.max(z, axis=0, keepdims=True) for z in parts])
    parts = [jnp.exp2(z - top) for z in parts]
    total = functools.reduce(jnp.add, [jnp.sum(z, axis=0, keepdims=True) for z in parts])
    inverse = 1.0 / total
    for j, z in enumerate(parts):
        wt_ref[0, j * 128 : (j + 1) * 128, :] = (z * inverse).astype(BF16)

    @pl.when(step == 0)
    def _():
        lgv_ref[...] = jnp.zeros_like(lgv_ref)

    for r in range(4):
        lgv_ref[r] += nn(wt_ref[0, r * ROWS : (r + 1) * ROWS, :], g)


def grad_kernel(
    aliased,
    wt_ref, k0, k1, k2, k3, v0, v1, v2, v3, l0, l1, l2, l3, cot_ref, g_ref, upq_ref, upv_ref, lowqt_ref, *rest
):
    att_ref, gu_ref, lgq_ref = rest[1:] if aliased else rest
    step = pl.program_id(0)
    cot = cot_ref[...]
    cot_g = jnp.concatenate([cot, g_ref[...]], axis=1)
    out_t = jnp.zeros((HD + R, ROWS), F32)
    dot_sum = jnp.zeros((1, ROWS), F32)
    backs = []
    for r, (v_ref, l_ref) in enumerate(((v0, l0), (v1, l1), (v2, l2), (v3, l3))):
        vl = jnp.concatenate([v_ref[...], l_ref[...]], axis=1)
        w = wt_ref[0, r * ROWS : (r + 1) * ROWS, :]
        back = nt(vl, cot_g)
        dot_sum += jnp.sum(w.astype(F32) * back, axis=0, keepdims=True)
        out_t += tn(vl, w)
        backs.append(back)
    dq_t = jnp.zeros((HD, ROWS), F32)
    for r, key_ref in enumerate((k0, k1, k2, k3)):
        w = wt_ref[0, r * ROWS : (r + 1) * ROWS, :].astype(F32)
        shifted = (w * (backs[r] - dot_sum)).astype(BF16)
        dq_t += tn(key_ref[...], shifted)
    dq_t = (dq_t * SCALE).astype(BF16)
    t1_t = out_t[HD:].astype(BF16)
    att_t = out_t[:HD] + tn(upv_ref[...], t1_t)
    att_ref[...] = att_t.T.astype(BF16)
    gu_ref[0, 0] = nt(lowqt_ref[...], dq_t).astype(BF16)
    gu_ref[0, 1] = nn(t1_t, cot).astype(BF16)

    @pl.when(step == 0)
    def _():
        lgq_ref[...] = jnp.zeros_like(lgq_ref)

    lgq_ref[...] += nn(upq_ref[...], dq_t)


def col(off):
    return pl.BlockSpec((ROWS, HD), lambda h: (0, h + off))


def colup(off):
    return pl.BlockSpec((R, HD), lambda h: (0, h + off))


def const(shape):
    return pl.BlockSpec(shape, lambda h: (0,) * len(shape))


def params():
    return pltpu.CompilerParams(dimension_semantics=("arbitrary",), vmem_limit_bytes=48 * 2**20)


def weight_call(h0, nh, bias, query_base, lowq, upq, cot, upv, own, sib, zs, zd):
    return pl.pallas_call(
        functools.partial(weight_kernel, h0),
        grid=(nh,),
        in_specs=[
            pl.BlockSpec(memory_space=pltpu.SMEM),
            col(h0), const((ROWS, R)), colup(h0), col(h0), colup(h0),
            col(h0), col(h0), col(0), col(0),
        ],
        out_specs=[
            pl.BlockSpec((1, 4 * ROWS, ROWS), lambda h: (h, 0, 0)),
            col(0),
            const((4, ROWS, R)),
        ],
        out_shape=[
            jax.ShapeDtypeStruct((nh, 4 * ROWS, ROWS), BF16),
            jax.ShapeDtypeStruct((ROWS, nh * HD), BF16),
            jax.ShapeDtypeStruct((4, ROWS, R), F32),
        ],
        compiler_params=params(),
        cost_estimate=pl.CostEstimate(
            flops=nh * 6 * 1024 * 256 * 128, bytes_accessed=nh * 1200000, transcendentals=nh * 1024 * 256
        ),
        name="attention_weights",
    )(bias, query_base, lowq, upq, cot, upv, own, sib, zs, zd)


def grad_call(h0, nh, kh0, kz, att, wt, k_own, k_sib, v_own, v_sib, vz, lows, cot, g, upq, upv, lowqt):
    aliased = att is not None
    args = [wt, k_own, k_sib, *kz, v_own, v_sib, *vz, *lows, cot, g, upq, upv, lowqt]
    off = h0 - kh0
    specs = [
        pl.BlockSpec((1, 4 * ROWS, ROWS), lambda h: (h + off, 0, 0)),
        col(h0), col(h0), col(off), col(off),
        col(h0), col(h0), col(0), col(0),
        *([const((ROWS, R))] * 4),
        col(h0), col(off), colup(h0), colup(h0), const((R, ROWS)),
    ]
    if aliased:
        args.append(att)
        specs.append(pl.BlockSpec(memory_space=pl.ANY))
    return pl.pallas_call(
        functools.partial(grad_kernel, aliased),
        grid=(nh,),
        in_specs=specs,
        out_specs=[
            col(h0),
            pl.BlockSpec((1, 2, R, HD), lambda h: (h, 0, 0, 0)),
            const((R, ROWS)),
        ],
        out_shape=[
            jax.ShapeDtypeStruct((ROWS, HEADS * HD), BF16),
            jax.ShapeDtypeStruct((nh, 2, R, HD), BF16),
            jax.ShapeDtypeStruct((R, ROWS), F32),
        ],
        input_output_aliases={len(args) - 1: 0} if aliased else {},
        compiler_params=params(),
        cost_estimate=pl.CostEstimate(
            flops=nh * 10 * 1024 * 256 * 128, bytes_accessed=nh * 1200000, transcendentals=0
        ),
        name="attention_grads",
    )(*args)


CORE_SWAP = [(0, 1), (1, 0)]


def over_core(a):
    return lax.ppermute(a, "core", CORE_SWAP)


def over_z(a):
    return lax.ppermute(a, "zl", CORE_SWAP)


def per_device(
    hidden, query_base, key_base, value_base, cotangent,
    down_query, down_value, up_query, up_value, key_blocks, block_counts,
):
    dp = lax.axis_size("dp")
    core = lax.axis_index("core")
    me = lax.axis_index("zl") * 2 + core

    def columns(a, h0, nh):
        return a[:, h0 * HD : (h0 + nh) * HD]

    k_zs = [over_z(columns(key_base, *c)) for c in K_CHUNKS]
    v_zs = [over_z(columns(value_base, *c)) for c in V_CHUNKS]
    k_sib = over_core(key_base)
    v_sib = over_core(value_base)
    k_zd = [over_core(a) for a in k_zs]
    v_zd = [over_core(a) for a in v_zs]

    listed = jnp.arange(key_blocks.shape[2])[None, None, :] < block_counts[:, :, None]
    allowed = jnp.any(
        (key_blocks[..., None] == jnp.arange(NB)) & listed[..., None], axis=2
    )
    bias = jnp.where(allowed, 0.0, -1e30).astype(F32)
    bias = lax.all_gather(bias, ("zl", "core"), axis=0, tiled=True)
    bias = lax.dynamic_slice_in_dim(bias, me * 2, 2, axis=1)
    source = (me ^ (jnp.arange(NB) // 2)) * 2 + jnp.arange(NB) % 2
    bias = jnp.sum(
        jnp.where(source[:, None] == jnp.arange(NB), bias[:, :, None, :], 0.0), axis=3
    ).reshape(HEADS, 2 * NB)

    low_query = nn(hidden, down_query).astype(BF16)
    low_value = nn(hidden, down_value).astype(BF16)
    lv_zs = over_z(low_value)
    lows = [low_value, over_core(low_value), lv_zs, over_core(lv_zs)]

    weights, gs, lgv = [], [], 0.0
    for (h0, nh), zs, zd in zip(K_CHUNKS, k_zs, k_zd):
        wt, g, part = weight_call(
            h0, nh, bias, query_base, low_query, up_query, cotangent, up_value, key_base, k_sib, zs, zd
        )
        weights.append(wt)
        gs.append(g)
        lgv = lgv + part

    near = lgv[0::2]
    chip = near + over_core(lgv[1::2].astype(BF16)).astype(F32)
    low_grad_value = chip[0] + over_z(chip[1].astype(BF16)).astype(F32)

    low_query_t = low_query.T
    att, gus, lgq = None, [], 0.0
    for (h0, nh), zs, zd in zip(V_CHUNKS, v_zs, v_zd):
        which = [i for i, (a, n) in enumerate(K_CHUNKS) if a <= h0 < a + n][0]
        att, gu, part = grad_call(
            h0, nh, K_CHUNKS[which][0], (k_zs[which], k_zd[which]), att, weights[which],
            key_base, k_sib, value_base, v_sib, (zs, zd), lows,
            cotangent, gs[which], up_query, up_value, low_query_t,
        )
        gus.append(gu)
        lgq = lgq + part

    low_grads = jnp.concatenate([lgq.T.astype(BF16), low_grad_value.astype(BF16)], axis=1)
    down = lax.dot_general(
        hidden, low_grads, (((0,), (0,)), ((), ())), preferred_element_type=F32
    ).astype(BF16)
    rows = hidden.shape[1] // (4 * dp)
    down = down.reshape(2 * dp, 2, rows, 2 * R)
    ups = [
        g.reshape(5, 2, dp, R // dp, HD).transpose(2, 0, 1, 3, 4).reshape(dp, -1, HD) for g in gus
    ]
    ups = jnp.stack(
        [jnp.stack([ups[0], ups[2]], axis=1), jnp.stack([ups[1], ups[3]], axis=1)], axis=0
    ).reshape(2, 2 * dp, -1, HD)
    down_mine = lax.dynamic_index_in_dim(down, core, 1, keepdims=False)
    down_other = lax.dynamic_index_in_dim(down, 1 - core, 1, keepdims=False)
    up_mine = lax.dynamic_index_in_dim(ups, core, 0, keepdims=False)
    up_other = lax.dynamic_index_in_dim(ups, 1 - core, 0, keepdims=False)
    down_sum = (down_mine.astype(F32) + over_core(down_other).astype(F32)).astype(BF16)
    up_sum = (up_mine.astype(F32) + over_core(up_other).astype(F32)).astype(BF16)
    n_up = up_sum.shape[1]
    payload = jnp.concatenate([down_sum.reshape(2 * dp, 2 * rows, R), up_sum], axis=1)
    landed = lax.all_to_all(payload, ("dp", "zl"), 0, 0, tiled=True)
    total = jnp.sum(landed.astype(F32), axis=0)
    grad_down = total[: 2 * rows].reshape(rows, 2, R)
    grad_up = (
        total[2 * rows :].reshape(5, 2, R // dp, HD).transpose(2, 1, 0, 3).reshape(R // dp, 2, 5 * HD)
    )
    return att, grad_down, grad_up


def solution(mesh):
    fine = Mesh(mesh.devices.reshape(-1, 2, 2), ("dp", "zl", "core"))
    everyone = ("dp", "zl", "core")
    tokens = P(everyone, None)
    return jax.shard_map(
        per_device,
        mesh=fine,
        in_specs=(
            tokens, tokens, tokens, tokens, tokens, P(), P(), P(), P(),
            P(("zl", "core"), None, None), P(("zl", "core"), None),
        ),
        out_specs=(tokens, P(everyone, None, None), P("dp", None, ("zl", "core"))),
        check_vma=False,
    )
```

```python
import functools
import math

import jax
import jax.numpy as jnp
from jax import lax
from jax.experimental import pallas as pl
from jax.experimental.pallas import tpu as pltpu
from jax.sharding import Mesh
from jax.sharding import PartitionSpec as P

HEADS = 20
HD = 128
R = 128
NB = 8
ROWS = 256
GH = 5
K_CHUNKS = ((0, 2), (2, 2))
V_CHUNKS = ((0, 2), (2, 2))
SCALE = 1.0 / math.sqrt(HD)
SCALE2 = SCALE * math.log2(math.e)
F32 = jnp.float32
BF16 = jnp.bfloat16


def nn(a, b):
    return lax.dot_general(a, b, (((1,), (0,)), ((), ())), preferred_element_type=F32)


def nt(a, b):
    return lax.dot_general(a, b, (((1,), (1,)), ((), ())), preferred_element_type=F32)


def tn(a, b):
    return lax.dot_general(a, b, (((0,), (0,)), ((), ())), preferred_element_type=F32)


def heads_of(h):
    return slice(h * HD, (h + 1) * HD)


def weight_kernel(
    chunk0, me_ref, bias_ref, qb_ref, lowq_ref, upq_ref, cot_ref, upv_ref, k0, k1, k2, k3, *rest
):
    step = pl.program_id(0)
    keys = (k0, k1, k2, k3)
    last_call = chunk0 > 0
    if last_call:
        before_ref, *rest = rest
    wt_ref, inv_ref, g_ref, *rest = rest
    if last_call:
        here_ref, sib_ref, zs_ref, zd_ref, *rest = rest
    lgv_ref, z_ref, q_ref = rest
    first_half = lax.broadcasted_iota(jnp.int32, (1, ROWS), 1) < ROWS // 2
    me = me_ref[0, 0]
    head0 = ((chunk0 + step) ^ me) * GH

    @pl.when(step == 0)
    def _():
        lgv_ref[...] = before_ref[...] if last_call else jnp.zeros_like(lgv_ref)

    tops, sums, scaled = [None] * GH, [None] * GH, [None] * GH

    def prepare(h):
        c = heads_of(h)
        q_ref[h % 2] = (qb_ref[:, c].astype(F32) + nn(lowq_ref[...], upq_ref[:, c])).astype(BF16)
        g_ref[:, c] = nt(cot_ref[:, c], upv_ref[:, c]).astype(BF16)

    def score(h, r):
        s = nt(keys[r][:, heads_of(h)], q_ref[h % 2]) * SCALE2
        for b in range(2):
            j = 2 * r + b
            block = (me ^ r) * 2 + b
            low, high = (bias_ref[head0 + h, (me * 2 + i) * NB + block] for i in range(2))
            z = s[b * 128 : (b + 1) * 128] + jnp.where(first_half, low, high)
            top = jnp.max(z.reshape(16, 8, ROWS), axis=0)
            tops[h] = top if tops[h] is None else jnp.maximum(tops[h], top)
            z_ref[h % 2, j * 128 : (j + 1) * 128] = z

    def power(h, r):
        if r == 0:
            tops[h] = jnp.max(tops[h], axis=0, keepdims=True)
        rows = slice(r * ROWS, (r + 1) * ROWS)
        p = jnp.exp2(z_ref[h % 2, rows] - tops[h])
        wt_ref[h, rows] = p.astype(BF16)
        part = jnp.sum(p.reshape(32, 8, ROWS), axis=0)
        sums[h] = part if sums[h] is None else sums[h] + part

    def finish(h):
        inv = 1.0 / jnp.sum(sums[h], axis=0, keepdims=True)
        inv_ref[h] = jnp.broadcast_to(inv, (8, ROWS))
        inv_rows = jnp.transpose(jnp.broadcast_to(inv, (R, ROWS)))
        scaled[h] = (g_ref[:, heads_of(h)].astype(F32) * inv_rows).astype(BF16)

    def low_grad(h, r):
        lgv_ref[r] += nn(wt_ref[h, r * ROWS : (r + 1) * ROWS], scaled[h])

    for i in range(GH + 2):
        if i < GH:
            prepare(i)
        for r in range(4):
            if i < GH:
                score(i, r)
            if 1 <= i <= GH:
                power(i - 1, r)
            if i >= 2:
                low_grad(i - 2, r)
        if 1 <= i <= GH:
            finish(i - 1)

    if last_call:

        @pl.when(step == pl.num_programs(0) - 1)
        def _():
            here_ref[...] = lgv_ref[0]
            for r, ref in enumerate((sib_ref, zs_ref, zd_ref)):
                ref[...] = lgv_ref[r + 1].astype(BF16)


def grad_kernel(
    aliased, downs,
    wt_ref, inv_ref, k0, k1, k2, k3, v0, v1, v2, v3, l0, l1, l2, l3,
    cot_ref, g_ref, upq_ref, upv_ref, lowqp_ref, perm_ref, *rest,
):
    rest = list(rest[1:] if aliased else rest)
    core_ref, *rest = rest
    if downs:
        hidden_ref, here_ref, *low_refs = rest[:6]
        rest = rest[6:]
    att_ref, lgq_ref, up_mine, up_other, *rest = rest
    if downs:
        down_mine, down_other, *rest = rest
    vl_ref, back_ref, sh_ref, gu_ref, up_ref, *rest = rest
    step = pl.program_id(0)
    first_step, last_step = step == 0, step == pl.num_programs(0) - 1
    if downs:
        held_ref, sem = rest
        fetch = pltpu.make_async_copy(hidden_ref, held_ref, sem)
        pl.when(first_step)(fetch.start)
    keys, vals, lows = (k0, k1, k2, k3), (v0, v1, v2, v3), (l0, l1, l2, l3)

    @pl.when(first_step)
    def _():
        lgq_ref[...] = jnp.zeros_like(lgq_ref)
        for p in range(2):
            for r in range(4):
                vl_ref[p, r * ROWS : (r + 1) * ROWS, HD:] = lows[r][...]

    cot_g, dots, outs, dqs = [None] * GH, [None] * GH, [None] * GH, [None] * GH

    def prepare(h):
        c = heads_of(h)
        cot_g[h] = jnp.concatenate([cot_ref[:, c], g_ref[:, c]], axis=1)
        for r in range(4):
            vl_ref[h % 2, r * ROWS : (r + 1) * ROWS, :HD] = vals[r][:, c]

    def back(h, r):
        rows = slice(r * ROWS, (r + 1) * ROWS)
        b = nt(vl_ref[h % 2, rows], cot_g[h])
        back_ref[h % 2, rows] = b
        part = jnp.sum((b * wt_ref[h, rows].astype(F32)).reshape(32, 8, ROWS), axis=0)
        dots[h] = part if dots[h] is None else dots[h] + part

    def shift(h, r):
        rows = slice(r * ROWS, (r + 1) * ROWS)
        if r == 0:
            dots[h] = jnp.sum(dots[h], axis=0, keepdims=True) * inv_ref[h, 0:1]
        sh_ref[h % 2, rows] = (
            wt_ref[h, rows].astype(F32) * (back_ref[h % 2, rows] - dots[h])
        ).astype(BF16)
        if r == 3:
            key = jnp.concatenate([k[:, heads_of(h)] for k in keys], axis=0)
            dqs[h] = tn(key, sh_ref[h % 2])

    def attend(h):
        outs[h] = tn(vl_ref[h % 2], wt_ref[h])

    def finish_out(h):
        c = heads_of(h)
        out = outs[h] * inv_ref[h, 0:1]
        t1 = out[HD:].astype(BF16)
        att_ref[:, c] = (out[:HD] + tn(upv_ref[:, c], t1)).T.astype(BF16)
        t1_rows = nn(perm_ref[...], t1).astype(BF16)
        gu_ref[1, :, c] = nn(t1_rows, cot_ref[:, c])

    def finish_query(h):
        dq = (dqs[h] * (inv_ref[h, 0:1] * SCALE)).astype(BF16)
        gu_ref[0, :, heads_of(h)] = nt(lowqp_ref[...], dq)
        lgq_ref[...] += nn(upq_ref[:, heads_of(h)], dq)

    for i in range(GH + 2):
        if i < GH:
            prepare(i)
        for r in range(4):
            if i < GH:
                back(i, r)
            if 1 <= i <= GH:
                shift(i - 1, r)
        if i < GH:
            attend(i)
        if 1 <= i <= GH:
            finish_out(i - 1)
        if i >= 2:
            finish_query(i - 2)

    dp, count, _ = up_mine.shape
    for i in range(count):
        which, row, h = i // (count // 2), i // GH % (R // dp), i % GH
        up_ref[step, :, i, :] = gu_ref[which, row * dp : (row + 1) * dp, heads_of(h)]

    @pl.when(last_step)
    def _():
        first = core_ref[0, 0] == 0
        up_mine[...] = jnp.where(first, up_ref[0], up_ref[1]).astype(BF16)
        up_other[...] = jnp.where(first, up_ref[1], up_ref[0]).astype(BF16)
        if downs:
            query = functools.reduce(jnp.add, [ref[...] for ref in low_refs[3:]], lgq_ref[...])
            value = functools.reduce(jnp.add, [ref[...].astype(F32) for ref in low_refs[:3]], here_ref[...])
            low = jnp.concatenate([query.T, value], axis=1).astype(BF16)
            fetch.wait()
            down(core_ref, held_ref, low, down_mine, down_other)


def down(core_ref, hidden_ref, low, mine_ref, other_ref):
    first = core_ref[0, 0] == 0
    dests, rows, _ = mine_ref.shape
    rows //= 2
    group = min(8, dests)
    for g in range(dests // group):
        res = tn(hidden_ref[:, 2 * rows * group * g : 2 * rows * group * (g + 1)], low)
        for d in range(group):
            a0 = res[2 * d * rows : (2 * d + 1) * rows]
            a1 = res[(2 * d + 1) * rows : (2 * d + 2) * rows]
            for ref, a in ((mine_ref, jnp.where(first, a0, a1)), (other_ref, jnp.where(first, a1, a0))):
                ref[g * group + d] = jnp.concatenate([a[:, :R], a[:, R:]], axis=0).astype(BF16)


def col(off):
    return pl.BlockSpec((ROWS, GH * HD), lambda i: (0, i + off))


def colup(off):
    return pl.BlockSpec((R, GH * HD), lambda i: (0, i + off))


def const(shape):
    return pl.BlockSpec(shape, lambda i: (0,) * len(shape))


def per_head(shape, off):
    return pl.BlockSpec((GH,) + shape, lambda i: (i + off,) + (0,) * len(shape))


def params():
    return pltpu.CompilerParams(dimension_semantics=("arbitrary",), vmem_limit_bytes=60 * 2**20)


def weight_call(c0, n, me, before, bias, query_base, lowq, upq, cot, upv, own, sib, zs, zd):
    keys = 4 * ROWS
    sums = jax.ShapeDtypeStruct((4, ROWS, R), F32)
    part = jax.ShapeDtypeStruct((ROWS, R), BF16)
    scratch = [pltpu.VMEM((2, keys, ROWS), F32), pltpu.VMEM((2, ROWS, HD), BF16)]
    if c0:
        extra, taken = [jax.ShapeDtypeStruct((ROWS, R), F32), part, part, part], [before]
        scratch = [pltpu.VMEM(sums.shape, F32), *scratch]
    else:
        extra, taken = [sums], []
    return pl.pallas_call(
        functools.partial(weight_kernel, c0),
        grid=(n,),
        in_specs=[
            pl.BlockSpec(memory_space=pltpu.SMEM),
            pl.BlockSpec(memory_space=pltpu.SMEM),
            col(c0), const((ROWS, R)), colup(c0), col(c0), colup(c0),
            col(c0), col(c0), col(0), col(0),
            *[const(sums.shape) for _ in taken],
        ],
        out_specs=[
            per_head((keys, ROWS), 0), per_head((8, ROWS), 0), col(0), *[const(out.shape) for out in extra],
        ],
        out_shape=[
            jax.ShapeDtypeStruct((n * GH, keys, ROWS), BF16),
            jax.ShapeDtypeStruct((n * GH, 8, ROWS), F32),
            jax.ShapeDtypeStruct((ROWS, n * GH * HD), BF16),
            *extra,
        ],
        scratch_shapes=scratch,
        compiler_params=params(),
        cost_estimate=pl.CostEstimate(
            flops=1_000_000, bytes_accessed=1_000, transcendentals=0
        ),
        name="attention_weights",
    )(me.reshape(1, 1), bias, query_base, lowq, upq, cot, upv, own, sib, zs, zd, *taken)


def grad_call(c0, n, kc0, core, att, wt, inv, keys, vals, lows, cot, g, upq, upv, lowqp, perm, dp, downs=None):
    off = c0 - kc0
    args = [wt, inv, *keys, *vals, *[low for low, _ in lows], cot, g, upq, upv, lowqp, perm]
    specs = [
        per_head((4 * ROWS, ROWS), off), per_head((8, ROWS), off),
        col(c0), col(c0), col(off), col(off),
        col(c0), col(c0), col(0), col(0),
        *[pl.BlockSpec((ROWS, R), functools.partial(lambda at, i: (0, at), at)) for _, at in lows],
        col(c0), col(off), colup(c0), colup(c0), const((R, ROWS)), const((R, R)),
    ]
    alias = {}
    if att is not None:
        alias = {len(args): 0}
        args.append(att)
        specs.append(pl.BlockSpec(memory_space=pl.ANY))
    args.append(core.reshape(1, 1))
    specs.append(pl.BlockSpec(memory_space=pltpu.SMEM))
    packed = (dp, 2 * (R // dp) * GH, HD)
    outs = [
        jax.ShapeDtypeStruct((ROWS, HEADS * HD), BF16),
        jax.ShapeDtypeStruct((R, ROWS), F32),
        jax.ShapeDtypeStruct(packed, BF16),
        jax.ShapeDtypeStruct(packed, BF16),
    ]
    out_specs = [col(c0), *[const(out.shape) for out in outs[1:]]]
    scratch = [
        pltpu.VMEM((2, 4 * ROWS, HD + R), BF16),
        pltpu.VMEM((2, 4 * ROWS, ROWS), F32),
        pltpu.VMEM((2, 4 * ROWS, ROWS), BF16),
        pltpu.VMEM((2, R, GH * HD), F32),
        pltpu.VMEM((n,) + packed, F32),
    ]
    if downs:
        hidden, *lows = downs
        args += [hidden, *lows]
        specs += [pl.BlockSpec(memory_space=pl.ANY), *[const(low.shape) for low in lows]]
        halves = (2 * dp, hidden.shape[1] // (2 * dp), R)
        outs += [jax.ShapeDtypeStruct(halves, BF16)] * 2
        out_specs += [const(halves)] * 2
        scratch += [pltpu.VMEM(hidden.shape, BF16), pltpu.SemaphoreType.DMA]
    return pl.pallas_call(
        functools.partial(grad_kernel, att is not None, bool(downs)),
        grid=(n,),
        in_specs=specs,
        out_specs=out_specs,
        out_shape=outs,
        scratch_shapes=scratch,
        input_output_aliases=alias,
        compiler_params=params(),
        cost_estimate=pl.CostEstimate(flops=1_000_000, bytes_accessed=1_000, transcendentals=0),
        name="attention_grads",
    )(*args)


DP = ("x", "zh", "y")
CORE_SWAP = [(0, 1), (1, 0)]


def over_core(a):
    return lax.ppermute(a, "core", CORE_SWAP)


def over_z(a):
    return lax.ppermute(a, "zl", CORE_SWAP)


def over_z_and_core(a):
    return lax.ppermute(a, ("zl", "core"), [(0, 3), (1, 2), (2, 1), (3, 0)])


def over_far_z(a):
    return lax.ppermute(a, ("zh", "zl"), [(0, 3), (1, 2), (2, 1), (3, 0)])


def per_device(
    hidden, query_base, key_base, value_base, cotangent,
    down_query, down_value, up_query, up_value, key_blocks, block_counts,
):
    dp = lax.axis_size(DP)
    core = lax.axis_index("core")
    me = lax.axis_index("zl") * 2 + core
    after = lax.optimization_barrier

    def columns(a, c0, n):
        return a[:, c0 * GH * HD : (c0 + n) * GH * HD]

    k_first = columns(key_base, *K_CHUNKS[0])
    key_rest, value_rest, key_blocks, block_counts, k_first = after(
        (key_base, value_base, key_blocks, block_counts, k_first)
    )
    k_zs = [over_z(k_first)]
    k_sib = over_core(key_rest)

    listed = jnp.arange(key_blocks.shape[2])[None, None, :] < block_counts[:, :, None]
    allowed = jnp.any((key_blocks[..., None] == jnp.arange(NB)) & listed[..., None], axis=2)
    bias = jnp.where(allowed, 0.0, -1e30).astype(F32).reshape(GH, NB * NB)
    bias = jnp.stack([bias, over_far_z(bias)])
    bias = jnp.stack([bias, over_core(bias)], axis=1).reshape(HEADS, NB * NB)

    low_value = nn(hidden, down_value).astype(BF16)
    low_query = nn(hidden, down_query).astype(BF16)
    key_rest, low_query = after((key_rest, low_query))
    k_second = columns(key_rest, *K_CHUNKS[1])
    v_first = jnp.concatenate([columns(value_rest, *V_CHUNKS[0]), low_value], axis=1)
    k_zs.append(over_z(k_second))
    k_zs[0], low_query, bias = after((k_zs[0], low_query, bias))
    k_zd = [over_core(k_zs[0])]
    v_zs = [over_z(v_first)]
    v_sib = over_core(value_base)
    low_sib = over_core(low_value)

    weights, lgv = [], [None]
    for i, (c0, n) in enumerate(K_CHUNKS):
        if i:
            value_rest, arrived, weights[-1] = after((value_rest, k_zs[i], weights[-1]))
            k_zd.append(over_core(arrived))
            v_zs.append(over_z(columns(value_rest, *V_CHUNKS[1])))
        wt, inv, g, *lgv = weight_call(
            c0, n, me, lgv[0], bias, query_base, low_query, up_query, cotangent, up_value,
            key_base, k_sib, k_zs[i], k_zd[i],
        )
        weights.append([wt, inv, g])
    lgv = [lgv[0], over_core(lgv[1]), over_z(lgv[2]), over_z_and_core(lgv[3])]

    att, lgqs, ups, v_zd = None, [], [], []
    for i, (c0, n) in enumerate(V_CHUNKS):
        which = [w for w, (a, m) in enumerate(K_CHUNKS) if a <= c0 < a + m][0]
        if i:
            arrived, att = after((v_zs[i], att))
        else:
            arrived, weights[-1], low_query, turn = after((v_zs[i], weights[-1], low_query, me * 0 + jnp.arange(R)))
            low_query_p = low_query.T.reshape(dp, R // dp, ROWS).transpose(1, 0, 2).reshape(R, ROWS)
            turn = turn % dp * (R // dp) + turn // dp
            perm = (turn[:, None] == jnp.arange(R)[None, :]).astype(BF16)
        v_zd.append(over_core(arrived))
        if not i:
            lows = [(low_value, 0), (low_sib, 0), (v_zs[0], 2 * GH), (v_zd[0], 2 * GH)]
        wt, inv, g = weights[which]
        att, lgq, *pair = grad_call(
            c0, n, K_CHUNKS[which][0], core, att, wt, inv,
            (key_base, k_sib, k_zs[which], k_zd[which]), (value_base, v_sib, v_zs[i], v_zd[i]),
            lows, cotangent, g, up_query, up_value, low_query_p, perm, dp,
            downs=(hidden, *lgv, *lgqs) if i else None,
        )
        lgqs.append(lgq)
        ups.append(pair)

    def both(mine, other):
        return (mine.astype(F32) + over_core(other).astype(F32)).astype(BF16)

    up = jnp.stack([both(*ups[0]), both(*ups[1][:2])], axis=1)
    down_sum = both(*ups[1][2:])
    payload = jnp.concatenate([down_sum, up.reshape(2 * dp, -1, HD)], axis=1)
    landed = lax.all_to_all(payload, DP + ("zl",), 0, 0, tiled=True)
    total = jnp.sum(landed.astype(F32), axis=0)
    rows = hidden.shape[1] // (4 * dp)
    grad_down = total[: 2 * rows].reshape(2, rows, R).transpose(1, 0, 2)
    grad_up = total[2 * rows :].reshape(2, R // dp, GH * HD).transpose(1, 0, 2)
    return att, grad_down, grad_up


def solution(mesh):
    dp = mesh.devices.shape[0]
    side = math.isqrt(dp // 2)
    fine = Mesh(mesh.devices.reshape(side, 2, side, 2, 2), DP + ("zl", "core"))
    everyone = DP + ("zl", "core")
    tokens = P(everyone, None)
    return jax.shard_map(
        per_device,
        mesh=fine,
        in_specs=(
            tokens, tokens, tokens, tokens, tokens, P(), P(), P(), P(),
            P(("zl", "core"), None, None), P(("zl", "core"), None),
        ),
        out_specs=(tokens, P(everyone, None, None), P(DP, None, ("zl", "core"))),
        check_vma=False,
    )
```

```python
import functools
import math

import jax
import jax.numpy as jnp
from jax import lax
from jax.experimental import pallas as pl
from jax.experimental.pallas import tpu as pltpu
from jax.sharding import Mesh
from jax.sharding import PartitionSpec as P

HEADS = 20
HD = 128
R = 128
NB = 8
ROWS = 256
GH = 5
K_CHUNKS = ((0, 2), (2, 2))
V_CHUNKS = ((0, 2), (2, 2))
SCALE = 1.0 / math.sqrt(HD)
SCALE2 = SCALE * math.log2(math.e)
F32 = jnp.float32
BF16 = jnp.bfloat16


def nn(a, b):
    return lax.dot_general(a, b, (((1,), (0,)), ((), ())), preferred_element_type=F32)


def nt(a, b):
    return lax.dot_general(a, b, (((1,), (1,)), ((), ())), preferred_element_type=F32)


def tn(a, b):
    return lax.dot_general(a, b, (((0,), (0,)), ((), ())), preferred_element_type=F32)


def heads_of(h):
    return slice(h * HD, (h + 1) * HD)


def weight_kernel(
    chunk0, me_ref, bias_ref, qb_ref, lowq_ref, upq_ref, cot_ref, upv_ref, k0, k1, k2, k3, *rest
):
    step = pl.program_id(0)
    keys = (k0, k1, k2, k3)
    last_call = chunk0 > 0
    if last_call:
        before_ref, *rest = rest
    wt_ref, inv_ref, g_ref, *rest = rest
    if last_call:
        here_ref, sib_ref, *rest = rest
    lgv_ref, z_ref, q_ref = rest
    first_half = lax.broadcasted_iota(jnp.int32, (1, ROWS), 1) < ROWS // 2
    me = me_ref[0, 0]
    head0 = ((chunk0 + step) ^ me) * GH

    @pl.when(step == 0)
    def _():
        lgv_ref[...] = before_ref[...] if last_call else jnp.zeros_like(lgv_ref)

    tops, sums, scaled = [None] * GH, [None] * GH, [None] * GH

    def prepare(h):
        c = heads_of(h)
        q_ref[h % 2] = (qb_ref[:, c].astype(F32) + nn(lowq_ref[...], upq_ref[:, c])).astype(BF16)
        g_ref[:, c] = nt(cot_ref[:, c], upv_ref[:, c]).astype(BF16)

    def score(h, r):
        s = nt(keys[r][:, heads_of(h)], q_ref[h % 2]) * SCALE2
        for b in range(2):
            j = 2 * r + b
            block = (me ^ r) * 2 + b
            low, high = (bias_ref[head0 + h, (me * 2 + i) * NB + block] for i in range(2))
            z = s[b * 128 : (b + 1) * 128] + jnp.where(first_half, low, high)
            top = jnp.max(z.reshape(16, 8, ROWS), axis=0)
            tops[h] = top if tops[h] is None else jnp.maximum(tops[h], top)
            z_ref[h % 2, j * 128 : (j + 1) * 128] = z

    def power(h, r):
        if r == 0:
            tops[h] = jnp.max(tops[h], axis=0, keepdims=True)
        rows = slice(r * ROWS, (r + 1) * ROWS)
        p = jnp.exp2(z_ref[h % 2, rows] - tops[h])
        wt_ref[h, rows] = p.astype(BF16)
        part = jnp.sum(p.reshape(32, 8, ROWS), axis=0)
        sums[h] = part if sums[h] is None else sums[h] + part

    def finish(h):
        inv = 1.0 / jnp.sum(sums[h], axis=0, keepdims=True)
        inv_ref[h] = jnp.broadcast_to(inv, (8, ROWS))
        inv_rows = jnp.transpose(jnp.broadcast_to(inv, (R, ROWS)))
        scaled[h] = (g_ref[:, heads_of(h)].astype(F32) * inv_rows).astype(BF16)

    def low_grad(h, r):
        lgv_ref[r] += nn(wt_ref[h, r * ROWS : (r + 1) * ROWS], scaled[h])

    for i in range(GH + 2):
        if i < GH:
            prepare(i)
        for r in range(4):
            if i < GH:
                score(i, r)
            if 1 <= i <= GH:
                power(i - 1, r)
            if i >= 2:
                low_grad(i - 2, r)
        if 1 <= i <= GH:
            finish(i - 1)

    if last_call:

        @pl.when(step == pl.num_programs(0) - 1)
        def _():
            for i in range(2):
                here_ref[i] = lgv_ref[2 * i]
                sib_ref[i] = lgv_ref[2 * i + 1].astype(BF16)


def grad_kernel(
    first_call, downs,
    wt_ref, inv_ref, k0, k1, k2, k3, v0, v1, v2, v3, l0, l1, l2, l3,
    cot_ref, g_ref, upq_ref, upv_ref, lowqp_ref, perm_ref, *rest,
):
    core_ref, *rest = rest[0 if first_call else 1 :]
    if first_call:
        near_ref, far_ref, *rest = rest
    if downs:
        hidden_ref, here_ref, there_ref, low_query_ref, *rest = rest
    att_ref, lgq_ref, up_mine, up_other, *rest = rest
    if first_call:
        here_ref, there_ref, *rest = rest
    if downs:
        down_mine, down_other, *rest = rest
    vl_ref, back_ref, sh_ref, gu_ref, up_ref, *rest = rest
    step = pl.program_id(0)
    first_step, last_step = step == 0, step == pl.num_programs(0) - 1
    if downs:
        held_ref, sem = rest
        fetch = pltpu.make_async_copy(hidden_ref, held_ref, sem)
        pl.when(first_step)(fetch.start)
    keys, vals, lows = (k0, k1, k2, k3), (v0, v1, v2, v3), (l0, l1, l2, l3)

    @pl.when(first_step)
    def _():
        lgq_ref[...] = jnp.zeros_like(lgq_ref)
        if first_call:
            here_ref[...] = near_ref[0] + far_ref[0].astype(F32)
            there_ref[...] = (near_ref[1] + far_ref[1].astype(F32)).astype(BF16)
        for p in range(2):
            for r in range(4):
                vl_ref[p, r * ROWS : (r + 1) * ROWS, HD:] = lows[r][...]

    cot_g, dots, outs, dqs = [None] * GH, [None] * GH, [None] * GH, [None] * GH

    def prepare(h):
        c = heads_of(h)
        cot_g[h] = jnp.concatenate([cot_ref[:, c], g_ref[:, c]], axis=1)
        for r in range(4):
            vl_ref[h % 2, r * ROWS : (r + 1) * ROWS, :HD] = vals[r][:, c]

    def back(h, r):
        rows = slice(r * ROWS, (r + 1) * ROWS)
        b = nt(vl_ref[h % 2, rows], cot_g[h])
        back_ref[h % 2, rows] = b
        part = jnp.sum((b * wt_ref[h, rows].astype(F32)).reshape(32, 8, ROWS), axis=0)
        dots[h] = part if dots[h] is None else dots[h] + part

    def shift(h, r):
        rows = slice(r * ROWS, (r + 1) * ROWS)
        if r == 0:
            dots[h] = jnp.sum(dots[h], axis=0, keepdims=True) * inv_ref[h, 0:1]
        sh_ref[h % 2, rows] = (
            wt_ref[h, rows].astype(F32) * (back_ref[h % 2, rows] - dots[h])
        ).astype(BF16)
        if r == 3:
            key = jnp.concatenate([k[:, heads_of(h)] for k in keys], axis=0)
            dqs[h] = tn(key, sh_ref[h % 2])

    def attend(h):
        outs[h] = tn(vl_ref[h % 2], wt_ref[h])

    def finish_out(h):
        c = heads_of(h)
        out = outs[h] * inv_ref[h, 0:1]
        t1 = out[HD:].astype(BF16)
        att_ref[:, c] = (out[:HD] + tn(upv_ref[:, c], t1)).T.astype(BF16)
        t1_rows = nn(perm_ref[...], t1).astype(BF16)
        gu_ref[1, :, c] = nn(t1_rows, cot_ref[:, c])

    def finish_query(h):
        dq = (dqs[h] * (inv_ref[h, 0:1] * SCALE)).astype(BF16)
        gu_ref[0, :, heads_of(h)] = nt(lowqp_ref[...], dq)
        lgq_ref[...] += nn(upq_ref[:, heads_of(h)], dq)

    for i in range(GH + 2):
        if i < GH:
            prepare(i)
        for r in range(4):
            if i < GH:
                back(i, r)
            if 1 <= i <= GH:
                shift(i - 1, r)
        if i < GH:
            attend(i)
        if 1 <= i <= GH:
            finish_out(i - 1)
        if i >= 2:
            finish_query(i - 2)

    dp, count, _ = up_mine.shape
    for i in range(count):
        which, row, h = i // (count // 2), i // GH % (R // dp), i % GH
        up_ref[step, :, i, :] = gu_ref[which, row * dp : (row + 1) * dp, heads_of(h)]

    @pl.when(last_step)
    def _():
        first = core_ref[0, 0] == 0
        up_mine[...] = jnp.where(first, up_ref[0], up_ref[1]).astype(BF16)
        up_other[...] = jnp.where(first, up_ref[1], up_ref[0]).astype(BF16)
        if downs:
            query = low_query_ref[...] + lgq_ref[...]
            value = here_ref[...] + there_ref[...].astype(F32)
            low = jnp.concatenate([query.T, value], axis=1).astype(BF16)
            fetch.wait()
            down(core_ref, held_ref, low, down_mine, down_other)


def down(core_ref, hidden_ref, low, mine_ref, other_ref):
    first = core_ref[0, 0] == 0
    dests, rows, _ = mine_ref.shape
    rows //= 2
    group = min(8, dests)
    for g in range(dests // group):
        res = tn(hidden_ref[:, 2 * rows * group * g : 2 * rows * group * (g + 1)], low)
        for d in range(group):
            a0 = res[2 * d * rows : (2 * d + 1) * rows]
            a1 = res[(2 * d + 1) * rows : (2 * d + 2) * rows]
            for ref, a in ((mine_ref, jnp.where(first, a0, a1)), (other_ref, jnp.where(first, a1, a0))):
                ref[g * group + d] = jnp.concatenate([a[:, :R], a[:, R:]], axis=0).astype(BF16)


def col(off):
    return pl.BlockSpec((ROWS, GH * HD), lambda i: (0, i + off))


def colup(off):
    return pl.BlockSpec((R, GH * HD), lambda i: (0, i + off))


def const(shape):
    return pl.BlockSpec(shape, lambda i: (0,) * len(shape))


def per_head(shape, off):
    return pl.BlockSpec((GH,) + shape, lambda i: (i + off,) + (0,) * len(shape))


def params():
    return pltpu.CompilerParams(dimension_semantics=("arbitrary",), vmem_limit_bytes=46 * 2**20)


def weight_call(c0, n, me, before, bias, query_base, lowq, upq, cot, upv, own, sib, zs, zd):
    keys = 4 * ROWS
    sums = jax.ShapeDtypeStruct((4, ROWS, R), F32)
    scratch = [pltpu.VMEM((2, keys, ROWS), F32), pltpu.VMEM((2, ROWS, HD), BF16)]
    if c0:
        extra, taken = [jax.ShapeDtypeStruct((2, ROWS, R), dtype) for dtype in (F32, BF16)], [before]
        scratch = [pltpu.VMEM(sums.shape, F32), *scratch]
    else:
        extra, taken = [sums], []
    return pl.pallas_call(
        functools.partial(weight_kernel, c0),
        grid=(n,),
        in_specs=[
            pl.BlockSpec(memory_space=pltpu.SMEM),
            pl.BlockSpec(memory_space=pltpu.SMEM),
            col(c0), const((ROWS, R)), colup(c0), col(c0), colup(c0),
            col(c0), col(c0), col(0), col(0),
            *[const(sums.shape) for _ in taken],
        ],
        out_specs=[
            per_head((keys, ROWS), 0), per_head((8, ROWS), 0), col(0), *[const(out.shape) for out in extra],
        ],
        out_shape=[
            jax.ShapeDtypeStruct((n * GH, keys, ROWS), BF16),
            jax.ShapeDtypeStruct((n * GH, 8, ROWS), F32),
            jax.ShapeDtypeStruct((ROWS, n * GH * HD), BF16),
            *extra,
        ],
        scratch_shapes=scratch,
        compiler_params=params(),
        cost_estimate=pl.CostEstimate(
            flops=1_000_000, bytes_accessed=1_000, transcendentals=0
        ),
        name="attention_weights",
    )(me.reshape(1, 1), bias, query_base, lowq, upq, cot, upv, own, sib, zs, zd, *taken)


def grad_call(c0, n, kc0, core, att, wt, inv, keys, vals, lows, cot, g, upq, upv, lowqp, perm, dp, low_sums, downs=None):
    off = c0 - kc0
    args = [wt, inv, *keys, *vals, *[low for low, _ in lows], cot, g, upq, upv, lowqp, perm]
    specs = [
        per_head((4 * ROWS, ROWS), off), per_head((8, ROWS), off),
        col(c0), col(c0), col(off), col(off),
        col(c0), col(c0), col(0), col(0),
        *[pl.BlockSpec((ROWS, R), functools.partial(lambda at, i: (0, at), at)) for _, at in lows],
        col(c0), col(off), colup(c0), colup(c0), const((R, ROWS)), const((R, R)),
    ]
    alias = {}
    if att is not None:
        alias = {len(args): 0}
        args.append(att)
        specs.append(pl.BlockSpec(memory_space=pl.ANY))
    args.append(core.reshape(1, 1))
    specs.append(pl.BlockSpec(memory_space=pltpu.SMEM))
    if not downs:
        args += low_sums
        specs += [const(low.shape) for low in low_sums]
    packed = (dp, 2 * (R // dp) * GH, HD)
    outs = [
        jax.ShapeDtypeStruct((ROWS, HEADS * HD), BF16),
        jax.ShapeDtypeStruct((R, ROWS), F32),
        jax.ShapeDtypeStruct(packed, BF16),
        jax.ShapeDtypeStruct(packed, BF16),
    ]
    if not downs:
        outs += [jax.ShapeDtypeStruct((ROWS, R), dtype) for dtype in (F32, BF16)]
    out_specs = [col(c0), *[const(out.shape) for out in outs[1:]]]
    scratch = [
        pltpu.VMEM((2, 4 * ROWS, HD + R), BF16),
        pltpu.VMEM((2, 4 * ROWS, ROWS), F32),
        pltpu.VMEM((2, 4 * ROWS, ROWS), BF16),
        pltpu.VMEM((2, R, GH * HD), F32),
        pltpu.VMEM((n,) + packed, F32),
    ]
    if downs:
        hidden, *lows = downs
        args += [hidden, *lows]
        specs += [pl.BlockSpec(memory_space=pl.ANY), *[const(low.shape) for low in lows]]
        halves = (2 * dp, hidden.shape[1] // (2 * dp), R)
        outs += [jax.ShapeDtypeStruct(halves, BF16)] * 2
        out_specs += [const(halves)] * 2
        scratch += [pltpu.VMEM(hidden.shape, BF16), pltpu.SemaphoreType.DMA]
    return pl.pallas_call(
        functools.partial(grad_kernel, att is None, bool(downs)),
        grid=(n,),
        in_specs=specs,
        out_specs=out_specs,
        out_shape=outs,
        scratch_shapes=scratch,
        input_output_aliases=alias,
        compiler_params=params(),
        cost_estimate=pl.CostEstimate(flops=1_000_000, bytes_accessed=1_000, transcendentals=0),
        name="attention_grads",
    )(*args)


DP = ("x", "zh", "y")
CORE_SWAP = [(0, 1), (1, 0)]


def over_core(a):
    return lax.ppermute(a, "core", CORE_SWAP)


def over_z(a):
    return lax.ppermute(a, "zl", CORE_SWAP)


def over_far_z(a):
    return lax.ppermute(a, ("zh", "zl"), [(0, 3), (1, 2), (2, 1), (3, 0)])


def per_device(
    hidden, query_base, key_base, value_base, cotangent,
    down_query, down_value, up_query, up_value, key_blocks, block_counts,
):
    dp = lax.axis_size(DP)
    core = lax.axis_index("core")
    me = lax.axis_index("zl") * 2 + core
    after = lax.optimization_barrier

    def columns(a, c0, n):
        return a[:, c0 * GH * HD : (c0 + n) * GH * HD]

    k_first = columns(key_base, *K_CHUNKS[0])
    key_rest, value_rest, key_blocks, block_counts, k_first = after(
        (key_base, value_base, key_blocks, block_counts, k_first)
    )
    k_zs = [over_z(k_first)]
    k_sib = over_core(key_rest)

    listed = jnp.arange(key_blocks.shape[2])[None, None, :] < block_counts[:, :, None]
    allowed = jnp.any((key_blocks[..., None] == jnp.arange(NB)) & listed[..., None], axis=2)
    bias = jnp.where(allowed, 0.0, -1e30).astype(F32).reshape(GH, NB * NB)
    bias = jnp.stack([bias, over_far_z(bias)])
    bias = jnp.stack([bias, over_core(bias)], axis=1).reshape(HEADS, NB * NB)

    low_value = nn(hidden, down_value).astype(BF16)
    low_query = nn(hidden, down_query).astype(BF16)
    key_rest, low_query = after((key_rest, low_query))
    k_second = columns(key_rest, *K_CHUNKS[1])
    v_first = jnp.concatenate([columns(value_rest, *V_CHUNKS[0]), low_value], axis=1)
    v_second = columns(value_rest, *V_CHUNKS[1])
    low_query_p = low_query.T.reshape(dp, R // dp, ROWS).transpose(1, 0, 2).reshape(R, ROWS)
    turn = jnp.arange(R)
    turn = turn % dp * (R // dp) + turn // dp
    perm = (turn[:, None] == jnp.arange(R)[None, :]).astype(BF16)
    k_zs[0], low_query, low_query_p, perm, bias, k_second, v_second = after(
        (k_zs[0], low_query, low_query_p, perm, bias, k_second, v_second)
    )
    k_zs.append(over_z(k_second))
    k_zd = [over_core(k_zs[0])]
    v_zs = [over_z(v_first)]
    v_sib = over_core(value_base)
    low_sib = over_core(low_value)

    weights, lgv = [], [None]
    for i, (c0, n) in enumerate(K_CHUNKS):
        if i:
            v_second, arrived, weights[-1] = after((v_second, k_zs[i], weights[-1]))
            k_zd.append(over_core(arrived))
            v_zs.append(over_z(v_second))
        wt, inv, g, *lgv = weight_call(
            c0, n, me, lgv[0], bias, query_base, low_query, up_query, cotangent, up_value,
            key_base, k_sib, k_zs[i], k_zd[i],
        )
        weights.append([wt, inv, g])
    near, far = lgv[0], over_core(lgv[1])

    def both(mine, other):
        return (mine.astype(F32) + over_core(other).astype(F32)).astype(BF16)

    att, v_zd = None, []
    for i, (c0, n) in enumerate(V_CHUNKS):
        which = [w for w, (a, m) in enumerate(K_CHUNKS) if a <= c0 < a + m][0]
        if i:
            arrived, att = after((v_zs[i], att))
        else:
            arrived, weights[-1] = after((v_zs[i], weights[-1]))
        v_zd.append(over_core(arrived))
        if not i:
            lows = [(low_value, 0), (low_sib, 0), (v_zs[0], 2 * GH), (v_zd[0], 2 * GH)]
        else:
            v_zd[i], up_first = after((v_zd[i], up_first))
        wt, inv, g = weights[which]
        att, *made = grad_call(
            c0, n, K_CHUNKS[which][0], core, att, wt, inv,
            (key_base, k_sib, k_zs[which], k_zd[which]), (value_base, v_sib, v_zs[i], v_zd[i]),
            lows, cotangent, g, up_query, up_value, low_query_p, perm, dp,
            (near, far), downs=(hidden, lgv_here, over_z(lgv_there), lgq) if i else None,
        )
        if not i:
            lgq, up_mine, up_other, lgv_here, lgv_there = made
            up_first = both(up_mine, up_other)
    up_mine, up_other, down_mine, down_other = made[1:]

    up = jnp.stack([up_first, both(up_mine, up_other)], axis=1)
    down_sum = both(down_mine, down_other)
    payload = jnp.concatenate([down_sum, up.reshape(2 * dp, -1, HD)], axis=1)
    landed = lax.all_to_all(payload, DP + ("zl",), 0, 0, tiled=True)
    total = jnp.sum(landed.astype(F32), axis=0)
    rows = hidden.shape[1] // (4 * dp)
    grad_down = total[: 2 * rows].reshape(2, rows, R).transpose(1, 0, 2)
    grad_up = total[2 * rows :].reshape(2, R // dp, GH * HD).transpose(1, 0, 2)
    return att, grad_down, grad_up


def solution(mesh):
    dp = mesh.devices.shape[0]
    side = math.isqrt(dp // 2)
    fine = Mesh(mesh.devices.reshape(side, 2, side, 2, 2), DP + ("zl", "core"))
    everyone = DP + ("zl", "core")
    tokens = P(everyone, None)
    return jax.shard_map(
        per_device,
        mesh=fine,
        in_specs=(
            tokens, tokens, tokens, tokens, tokens, P(), P(), P(), P(),
            P(("zl", "core"), None, None), P(("zl", "core"), None),
        ),
        out_specs=(tokens, P(everyone, None, None), P(DP, None, ("zl", "core"))),
        check_vma=False,
    )
```

```python
import functools
import math

import jax
import jax.numpy as jnp
from jax import lax
from jax.experimental import pallas as pl
from jax.experimental.pallas import tpu as pltpu
from jax.sharding import Mesh
from jax.sharding import PartitionSpec as P

HEADS = 20
HD = 128
R = 128
NB = 8
ROWS = 256
GH = 5
K_CHUNKS = ((0, 2), (2, 2))
V_CHUNKS = ((0, 2), (2, 2))
SCALE = 1.0 / math.sqrt(HD)
SCALE2 = SCALE * math.log2(math.e)
F32 = jnp.float32
BF16 = jnp.bfloat16


def nn(a, b):
    return lax.dot_general(a, b, (((1,), (0,)), ((), ())), preferred_element_type=F32)


def nt(a, b):
    return lax.dot_general(a, b, (((1,), (1,)), ((), ())), preferred_element_type=F32)


def tn(a, b):
    return lax.dot_general(a, b, (((0,), (0,)), ((), ())), preferred_element_type=F32)


def low_kernel(hidden_ref, down_query_ref, down_value_ref, query_ref, value_ref):
    query_ref[...] = nn(hidden_ref[...], down_query_ref[...]).astype(BF16)
    value_ref[...] = nn(hidden_ref[...], down_value_ref[...]).astype(BF16)


def heads_of(h):
    return slice(h * HD, (h + 1) * HD)


def of_step(a_ref, b_ref, cols):
    return jnp.where(pl.program_id(0) == 0, a_ref[:, cols], b_ref[:, cols])


def weight_kernel(
    chunk0, me_ref, bias_ref, qb_ref, lowq_ref, upq_ref, cot_ref, upv_ref, k0, k1, k2a, k2b, k3a, k3b, *rest
):
    step = pl.program_id(0)
    keys = (
        lambda c: k0[:, c], lambda c: k1[:, c],
        functools.partial(of_step, k2a, k2b), functools.partial(of_step, k3a, k3b),
    )
    last_call = chunk0 > 0
    if last_call:
        before_ref, *rest = rest
    wt_ref, inv_ref, g_ref, *rest = rest
    if last_call:
        here_ref, sib_ref, *rest = rest
    lgv_ref, z_ref, q_ref = rest
    first_half = lax.broadcasted_iota(jnp.int32, (1, ROWS), 1) < ROWS // 2
    me = me_ref[0, 0]
    head0 = ((chunk0 + step) ^ me) * GH

    @pl.when(step == 0)
    def _():
        lgv_ref[...] = before_ref[...] if last_call else jnp.zeros_like(lgv_ref)

    tops, sums, scaled = [None] * GH, [None] * GH, [None] * GH

    def prepare(h):
        c = heads_of(h)
        q_ref[h % 2] = (qb_ref[:, c].astype(F32) + nn(lowq_ref[...], upq_ref[:, c])).astype(BF16)
        g_ref[:, c] = nt(cot_ref[:, c], upv_ref[:, c]).astype(BF16)

    def score(h, r):
        s = nt(keys[r](heads_of(h)), q_ref[h % 2]) * SCALE2
        for b in range(2):
            j = 2 * r + b
            block = (me ^ r) * 2 + b
            low, high = (bias_ref[head0 + h, (me * 2 + i) * NB + block] for i in range(2))
            z = s[b * 128 : (b + 1) * 128] + jnp.where(first_half, low, high)
            top = jnp.max(z.reshape(16, 8, ROWS), axis=0)
            tops[h] = top if tops[h] is None else jnp.maximum(tops[h], top)
            z_ref[h % 2, j * 128 : (j + 1) * 128] = z

    def power(h, r):
        if r == 0:
            tops[h] = jnp.max(tops[h], axis=0, keepdims=True)
        rows = slice(r * ROWS, (r + 1) * ROWS)
        p = jnp.exp2(z_ref[h % 2, rows] - tops[h])
        wt_ref[h, rows] = p.astype(BF16)
        part = jnp.sum(p.reshape(32, 8, ROWS), axis=0)
        sums[h] = part if sums[h] is None else sums[h] + part

    def finish(h):
        inv = 1.0 / jnp.sum(sums[h], axis=0, keepdims=True)
        inv_ref[h] = jnp.broadcast_to(inv, (8, ROWS))
        inv_rows = jnp.transpose(jnp.broadcast_to(inv, (R, ROWS)))
        scaled[h] = (g_ref[:, heads_of(h)].astype(F32) * inv_rows).astype(BF16)

    def low_grad(h, r):
        lgv_ref[r] += nn(wt_ref[h, r * ROWS : (r + 1) * ROWS], scaled[h])

    for i in range(GH + 2):
        if i < GH:
            prepare(i)
        for r in range(4):
            if i < GH:
                score(i, r)
            if 1 <= i <= GH:
                power(i - 1, r)
            if i >= 2:
                low_grad(i - 2, r)
        if 1 <= i <= GH:
            finish(i - 1)

    if last_call:

        @pl.when(step == pl.num_programs(0) - 1)
        def _():
            for i in range(2):
                here_ref[i] = lgv_ref[2 * i]
                sib_ref[i] = lgv_ref[2 * i + 1].astype(BF16)


def grad_kernel(
    first_call, downs,
    wt_ref, inv_ref, k0, k1, k2a, k2b, k3a, k3b, v0, v1, v2a, v2b, v3a, v3b, l0, l1, l2, l3,
    cot_ref, g_ref, upq_ref, upv_ref, lowqp_ref, perm_ref, *rest,
):
    core_ref, *rest = rest[0 if first_call else 1 :]
    if first_call:
        near_ref, far_ref, *rest = rest
    if downs:
        hidden_ref, here_ref, there_ref, low_query_ref, *rest = rest
    att_ref, lgq_ref, up_mine, up_other, *rest = rest
    if first_call:
        here_ref, there_ref, *rest = rest
    if downs:
        down_mine, down_other, *rest = rest
    vl_ref, back_ref, sh_ref, gu_ref, up_ref, *rest = rest
    step = pl.program_id(0)
    first_step, last_step = step == 0, step == pl.num_programs(0) - 1
    if downs:
        held_ref, sem = rest
        fetch = pltpu.make_async_copy(hidden_ref, held_ref, sem)
        pl.when(first_step)(fetch.start)
    keys = (
        lambda c: k0[:, c], lambda c: k1[:, c],
        functools.partial(of_step, k2a, k2b), functools.partial(of_step, k3a, k3b),
    )
    vals = (
        lambda c: v0[:, c], lambda c: v1[:, c],
        functools.partial(of_step, v2a, v2b), functools.partial(of_step, v3a, v3b),
    )
    lows = (l0, l1, l2, l3)

    @pl.when(first_step)
    def _():
        lgq_ref[...] = jnp.zeros_like(lgq_ref)
        if first_call:
            here_ref[...] = near_ref[0] + far_ref[0].astype(F32)
            there_ref[...] = (near_ref[1] + far_ref[1].astype(F32)).astype(BF16)
        for p in range(2):
            for r in range(4):
                vl_ref[p, r * ROWS : (r + 1) * ROWS, HD:] = lows[r][...]

    cot_g, dots, outs, dqs = [None] * GH, [None] * GH, [None] * GH, [None] * GH

    def prepare(h):
        c = heads_of(h)
        cot_g[h] = jnp.concatenate([cot_ref[:, c], g_ref[:, c]], axis=1)
        for r in range(4):
            vl_ref[h % 2, r * ROWS : (r + 1) * ROWS, :HD] = vals[r](c)

    def back(h, r):
        rows = slice(r * ROWS, (r + 1) * ROWS)
        b = nt(vl_ref[h % 2, rows], cot_g[h])
        back_ref[h % 2, rows] = b
        part = jnp.sum((b * wt_ref[h, rows].astype(F32)).reshape(32, 8, ROWS), axis=0)
        dots[h] = part if dots[h] is None else dots[h] + part

    def shift(h, r):
        rows = slice(r * ROWS, (r + 1) * ROWS)
        if r == 0:
            dots[h] = jnp.sum(dots[h], axis=0, keepdims=True) * inv_ref[h, 0:1]
        sh_ref[h % 2, rows] = (
            wt_ref[h, rows].astype(F32) * (back_ref[h % 2, rows] - dots[h])
        ).astype(BF16)
        if r == 3:
            key = jnp.concatenate([k(heads_of(h)) for k in keys], axis=0)
            dqs[h] = tn(key, sh_ref[h % 2])

    def attend(h):
        outs[h] = tn(vl_ref[h % 2], wt_ref[h])

    def finish_out(h):
        c = heads_of(h)
        out = outs[h] * inv_ref[h, 0:1]
        t1 = out[HD:].astype(BF16)
        att_ref[:, c] = (out[:HD] + tn(upv_ref[:, c], t1)).T.astype(BF16)
        t1_rows = nn(perm_ref[...], t1).astype(BF16)
        gu_ref[1, :, c] = nn(t1_rows, cot_ref[:, c])

    def finish_query(h):
        dq = (dqs[h] * (inv_ref[h, 0:1] * SCALE)).astype(BF16)
        gu_ref[0, :, heads_of(h)] = nt(lowqp_ref[...], dq)
        lgq_ref[...] += nn(upq_ref[:, heads_of(h)], dq)

    for i in range(GH + 2):
        if i < GH:
            prepare(i)
        for r in range(4):
            if i < GH:
                back(i, r)
            if 1 <= i <= GH:
                shift(i - 1, r)
        if i < GH:
            attend(i)
        if 1 <= i <= GH:
            finish_out(i - 1)
        if i >= 2:
            finish_query(i - 2)

    dp, count, _ = up_mine.shape
    for i in range(count):
        which, row, h = i // (count // 2), i // GH % (R // dp), i % GH
        up_ref[step, :, i, :] = gu_ref[which, row * dp : (row + 1) * dp, heads_of(h)]

    @pl.when(last_step)
    def _():
        first = core_ref[0, 0] == 0
        up_mine[...] = jnp.where(first, up_ref[0], up_ref[1]).astype(BF16)
        up_other[...] = jnp.where(first, up_ref[1], up_ref[0]).astype(BF16)
        if downs:
            query = low_query_ref[...] + lgq_ref[...]
            value = here_ref[...] + there_ref[...].astype(F32)
            low = jnp.concatenate([query.T, value], axis=1).astype(BF16)
            fetch.wait()
            down(core_ref, held_ref, low, down_mine, down_other)


def down(core_ref, hidden_ref, low, mine_ref, other_ref):
    first = core_ref[0, 0] == 0
    dests, rows, _ = mine_ref.shape
    rows //= 2
    group = min(8, dests)
    for g in range(dests // group):
        res = tn(hidden_ref[:, 2 * rows * group * g : 2 * rows * group * (g + 1)], low)
        for d in range(group):
            a0 = res[2 * d * rows : (2 * d + 1) * rows]
            a1 = res[(2 * d + 1) * rows : (2 * d + 2) * rows]
            for ref, a in ((mine_ref, jnp.where(first, a0, a1)), (other_ref, jnp.where(first, a1, a0))):
                ref[g * group + d] = jnp.concatenate([a[:, :R], a[:, R:]], axis=0).astype(BF16)


def col(off):
    return pl.BlockSpec((ROWS, GH * HD), lambda i: (0, i + off))


def group():
    return pl.BlockSpec((ROWS, GH * HD), lambda i: (0, 0))


def colup(off):
    return pl.BlockSpec((R, GH * HD), lambda i: (0, i + off))


def const(shape):
    return pl.BlockSpec(shape, lambda i: (0,) * len(shape))


def per_head(shape, off):
    return pl.BlockSpec((GH,) + shape, lambda i: (i + off,) + (0,) * len(shape))


def params():
    return pltpu.CompilerParams(dimension_semantics=("arbitrary",), vmem_limit_bytes=46 * 2**20)


def low_call(hidden, down_query, down_value):
    out = jax.ShapeDtypeStruct((ROWS, R), BF16)
    return pl.pallas_call(
        low_kernel,
        grid=(1,),
        in_specs=[const(hidden.shape), const(down_query.shape), const(down_value.shape)],
        out_specs=[const(out.shape)] * 2,
        out_shape=[out, out],
        compiler_params=params(),
        cost_estimate=pl.CostEstimate(flops=1_000_000, bytes_accessed=1_000, transcendentals=0),
        name="low_products",
    )(hidden, down_query, down_value)


def weight_call(c0, n, me, before, bias, query_base, lowq, upq, cot, upv, own, sib, zs, zd):
    keys = 4 * ROWS
    sums = jax.ShapeDtypeStruct((4, ROWS, R), F32)
    scratch = [pltpu.VMEM((2, keys, ROWS), F32), pltpu.VMEM((2, ROWS, HD), BF16)]
    if c0:
        extra, taken = [jax.ShapeDtypeStruct((2, ROWS, R), dtype) for dtype in (F32, BF16)], [before]
        scratch = [pltpu.VMEM(sums.shape, F32), *scratch]
    else:
        extra, taken = [sums], []
    return pl.pallas_call(
        functools.partial(weight_kernel, c0),
        grid=(n,),
        in_specs=[
            pl.BlockSpec(memory_space=pltpu.SMEM),
            pl.BlockSpec(memory_space=pltpu.SMEM),
            col(c0), const((ROWS, R)), colup(c0), col(c0), colup(c0),
            col(c0), col(c0), group(), group(), group(), group(),
            *[const(sums.shape) for _ in taken],
        ],
        out_specs=[
            per_head((keys, ROWS), 0), per_head((8, ROWS), 0), col(0), *[const(out.shape) for out in extra],
        ],
        out_shape=[
            jax.ShapeDtypeStruct((n * GH, keys, ROWS), BF16),
            jax.ShapeDtypeStruct((n * GH, 8, ROWS), F32),
            jax.ShapeDtypeStruct((ROWS, n * GH * HD), BF16),
            *extra,
        ],
        scratch_shapes=scratch,
        compiler_params=params(),
        cost_estimate=pl.CostEstimate(
            flops=1_000_000, bytes_accessed=1_000, transcendentals=0
        ),
        name="attention_weights",
    )(me.reshape(1, 1), bias, query_base, lowq, upq, cot, upv, own, sib, *zs, *zd, *taken)


def grad_call(c0, n, kc0, core, att, wt, inv, keys, vals, lows, cot, g, upq, upv, lowqp, perm, dp, low_sums, downs=None):
    off = c0 - kc0
    args = [wt, inv, *keys, *vals, *[low for low, _ in lows], cot, g, upq, upv, lowqp, perm]
    specs = [
        per_head((4 * ROWS, ROWS), off), per_head((8, ROWS), off),
        col(c0), col(c0), group(), group(), group(), group(),
        col(c0), col(c0), group(), group(), group(), group(),
        *[pl.BlockSpec((ROWS, R), functools.partial(lambda at, i: (0, at), at)) for _, at in lows],
        col(c0), col(off), colup(c0), colup(c0), const((R, ROWS)), const((R, R)),
    ]
    alias = {}
    if att is not None:
        alias = {len(args): 0}
        args.append(att)
        specs.append(pl.BlockSpec(memory_space=pl.ANY))
    args.append(core.reshape(1, 1))
    specs.append(pl.BlockSpec(memory_space=pltpu.SMEM))
    if not downs:
        args += low_sums
        specs += [const(low.shape) for low in low_sums]
    packed = (dp, 2 * (R // dp) * GH, HD)
    outs = [
        jax.ShapeDtypeStruct((ROWS, HEADS * HD), BF16),
        jax.ShapeDtypeStruct((R, ROWS), F32),
        jax.ShapeDtypeStruct(packed, BF16),
        jax.ShapeDtypeStruct(packed, BF16),
    ]
    if not downs:
        outs += [jax.ShapeDtypeStruct((ROWS, R), dtype) for dtype in (F32, BF16)]
    out_specs = [col(c0), *[const(out.shape) for out in outs[1:]]]
    scratch = [
        pltpu.VMEM((2, 4 * ROWS, HD + R), BF16),
        pltpu.VMEM((2, 4 * ROWS, ROWS), F32),
        pltpu.VMEM((2, 4 * ROWS, ROWS), BF16),
        pltpu.VMEM((2, R, GH * HD), F32),
        pltpu.VMEM((n,) + packed, F32),
    ]
    if downs:
        hidden, *lows = downs
        args += [hidden, *lows]
        specs += [pl.BlockSpec(memory_space=pl.ANY), *[const(low.shape) for low in lows]]
        halves = (2 * dp, hidden.shape[1] // (2 * dp), R)
        outs += [jax.ShapeDtypeStruct(halves, BF16)] * 2
        out_specs += [const(halves)] * 2
        scratch += [pltpu.VMEM(hidden.shape, BF16), pltpu.SemaphoreType.DMA]
    return pl.pallas_call(
        functools.partial(grad_kernel, att is None, bool(downs)),
        grid=(n,),
        in_specs=specs,
        out_specs=out_specs,
        out_shape=outs,
        scratch_shapes=scratch,
        input_output_aliases=alias,
        compiler_params=params(),
        cost_estimate=pl.CostEstimate(flops=1_000_000, bytes_accessed=1_000, transcendentals=0),
        name="attention_grads",
    )(*args)


DP = ("x", "zh", "y")
CORE_SWAP = [(0, 1), (1, 0)]


def over_core(a):
    return lax.ppermute(a, "core", CORE_SWAP)


def over_z(a):
    return lax.ppermute(a, "zl", CORE_SWAP)


def over_far_z(a):
    return lax.ppermute(a, ("zh", "zl"), [(0, 3), (1, 2), (2, 1), (3, 0)])


def per_device(
    hidden, query_base, key_base, value_base, cotangent,
    down_query, down_value, up_query, up_value, key_blocks, block_counts,
):
    dp = lax.axis_size(DP)
    core = lax.axis_index("core")
    me = lax.axis_index("zl") * 2 + core
    after = lax.optimization_barrier

    def columns(a, c0, n):
        return a[:, c0 * GH * HD : (c0 + n) * GH * HD]

    k_first = tuple(columns(key_base, g, 1) for g in (0, 1))
    key_rest, value_rest, k_first = after((key_base, value_base, k_first))
    k_zs = [tuple(over_z(a) for a in k_first)]
    k_sib = over_core(key_rest)
    k_sib, hidden, key_blocks, block_counts = after((k_sib, hidden, key_blocks, block_counts))

    listed = jnp.arange(key_blocks.shape[2])[None, None, :] < block_counts[:, :, None]
    allowed = jnp.any((key_blocks[..., None] == jnp.arange(NB)) & listed[..., None], axis=2)
    bias = jnp.where(allowed, 0.0, -1e30).astype(F32).reshape(GH, NB * NB)
    bias = jnp.stack([bias, over_far_z(bias)])
    bias = jnp.stack([bias, over_core(bias)], axis=1).reshape(HEADS, NB * NB)

    low_query, low_value = low_call(hidden, down_query, down_value)
    key_rest, low_query = after((key_rest, low_query))
    k_second = tuple(columns(key_rest, g, 1) for g in (2, 3))
    v_first = (jnp.concatenate([columns(value_rest, 0, 1), low_value], axis=1), columns(value_rest, 1, 1))
    v_second = tuple(columns(value_rest, g, 1) for g in (2, 3))
    low_query_p = low_query.T.reshape(dp, R // dp, ROWS).transpose(1, 0, 2).reshape(R, ROWS)
    turn = jnp.arange(R)
    turn = turn % dp * (R // dp) + turn // dp
    perm = (turn[:, None] == jnp.arange(R)[None, :]).astype(BF16)
    k_zs[0], low_query, low_query_p, perm, bias, k_second, v_second = after(
        (k_zs[0], low_query, low_query_p, perm, bias, k_second, v_second)
    )
    k_zs.append(tuple(over_z(a) for a in k_second))
    k_zd = [tuple(over_core(a) for a in k_zs[0])]
    v_zs = [tuple(over_z(a) for a in v_first)]
    v_sib = over_core(value_base)
    low_sib = over_core(low_value)

    weights, lgv = [], [None]
    for i, (c0, n) in enumerate(K_CHUNKS):
        if i:
            v_second, arrived, weights[-1] = after((v_second, k_zs[i], weights[-1]))
            k_zd.append(tuple(over_core(a) for a in arrived))
            v_zs.append(tuple(over_z(a) for a in v_second))
        wt, inv, g, *lgv = weight_call(
            c0, n, me, lgv[0], bias, query_base, low_query, up_query, cotangent, up_value,
            key_base, k_sib, k_zs[i], k_zd[i],
        )
        weights.append([wt, inv, g])
    near, far = lgv[0], over_core(lgv[1])

    def both(mine, other):
        return (mine.astype(F32) + over_core(other).astype(F32)).astype(BF16)

    att, v_zd = None, []
    for i, (c0, n) in enumerate(V_CHUNKS):
        which = [w for w, (a, m) in enumerate(K_CHUNKS) if a <= c0 < a + m][0]
        if i:
            arrived, att = after((v_zs[i], att))
        else:
            arrived, weights[-1] = after((v_zs[i], weights[-1]))
        v_zd.append(tuple(over_core(a) for a in arrived))
        if not i:
            lows = [(low_value, 0), (low_sib, 0), (v_zs[0][0], GH), (v_zd[0][0], GH)]
        else:
            v_zd[i], up_first = after((v_zd[i], up_first))
        wt, inv, g = weights[which]
        att, *made = grad_call(
            c0, n, K_CHUNKS[which][0], core, att, wt, inv,
            (key_base, k_sib, *k_zs[which], *k_zd[which]), (value_base, v_sib, *v_zs[i], *v_zd[i]),
            lows, cotangent, g, up_query, up_value, low_query_p, perm, dp,
            (near, far), downs=(hidden, lgv_here, over_z(lgv_there), lgq) if i else None,
        )
        if not i:
            lgq, up_mine, up_other, lgv_here, lgv_there = made
            up_first = both(up_mine, up_other)
    up_mine, up_other, down_mine, down_other = made[1:]

    up = jnp.stack([up_first, both(up_mine, up_other)], axis=1)
    down_sum = both(down_mine, down_other)
    payload = jnp.concatenate([down_sum, up.reshape(2 * dp, -1, HD)], axis=1)
    landed = lax.all_to_all(payload, DP + ("zl",), 0, 0, tiled=True)
    total = jnp.sum(landed.astype(F32), axis=0)
    rows = hidden.shape[1] // (4 * dp)
    grad_down = total[: 2 * rows].reshape(2, rows, R).transpose(1, 0, 2)
    grad_up = total[2 * rows :].reshape(2, R // dp, GH * HD).transpose(1, 0, 2)
    return att, grad_down, grad_up


def solution(mesh):
    dp = mesh.devices.shape[0]
    side = math.isqrt(dp // 2)
    fine = Mesh(mesh.devices.reshape(side, 2, side, 2, 2), DP + ("zl", "core"))
    everyone = DP + ("zl", "core")
    tokens = P(everyone, None)
    return jax.shard_map(
        per_device,
        mesh=fine,
        in_specs=(
            tokens, tokens, tokens, tokens, tokens, P(), P(), P(), P(),
            P(("zl", "core"), None, None), P(("zl", "core"), None),
        ),
        out_specs=(tokens, P(everyone, None, None), P(DP, None, ("zl", "core"))),
        check_vma=False,
    )
```

```python
import functools
import math

import jax
import jax.numpy as jnp
from jax import lax
from jax.experimental import pallas as pl
from jax.experimental.pallas import tpu as pltpu
from jax.sharding import Mesh
from jax.sharding import PartitionSpec as P

HEADS = 20
HD = 128
R = 128
NB = 8
ROWS = 256
GH = 5
K_CHUNKS = ((0, 2), (2, 2))
V_CHUNKS = ((0, 2), (2, 2))
SCALE = 1.0 / math.sqrt(HD)
SCALE2 = SCALE * math.log2(math.e)
F32 = jnp.float32
BF16 = jnp.bfloat16


def nn(a, b):
    return lax.dot_general(a, b, (((1,), (0,)), ((), ())), preferred_element_type=F32)


def nt(a, b):
    return lax.dot_general(a, b, (((1,), (1,)), ((), ())), preferred_element_type=F32)


def tn(a, b):
    return lax.dot_general(a, b, (((0,), (0,)), ((), ())), preferred_element_type=F32)


def low_kernel(hidden_ref, down_query_ref, down_value_ref, query_ref, value_ref):
    query_ref[...] = nn(hidden_ref[...], down_query_ref[...]).astype(BF16)
    value_ref[...] = nn(hidden_ref[...], down_value_ref[...]).astype(BF16)


def heads_of(h):
    return slice(h * HD, (h + 1) * HD)


def of_step(a_ref, b_ref, cols):
    return jnp.where(pl.program_id(0) == 0, a_ref[:, cols], b_ref[:, cols])


def weight_kernel(
    chunk0, me_ref, bias_ref, qb_ref, lowq_ref, upq_ref, cot_ref, upv_ref, k0, k1, k2a, k2b, k3a, k3b, *rest
):
    step = pl.program_id(0)
    keys = (
        lambda c: k0[:, c], lambda c: k1[:, c],
        functools.partial(of_step, k2a, k2b), functools.partial(of_step, k3a, k3b),
    )
    last_call = chunk0 > 0
    if last_call:
        before_ref, *rest = rest
    wt_ref, inv_ref, g_ref, *rest = rest
    if last_call:
        here_ref, sib_ref, *rest = rest
    lgv_ref, z_ref, q_ref = rest
    first_half = lax.broadcasted_iota(jnp.int32, (1, ROWS), 1) < ROWS // 2
    me = me_ref[0, 0]
    head0 = ((chunk0 + step) ^ me) * GH

    @pl.when(step == 0)
    def _():
        lgv_ref[...] = before_ref[...] if last_call else jnp.zeros_like(lgv_ref)

    tops, sums, scaled = [None] * GH, [None] * GH, [None] * GH

    def prepare(h):
        c = heads_of(h)
        q_ref[h % 2] = (qb_ref[:, c].astype(F32) + nn(lowq_ref[...], upq_ref[:, c])).astype(BF16)
        g_ref[:, c] = nt(cot_ref[:, c], upv_ref[:, c]).astype(BF16)

    def score(h, r):
        s = nt(keys[r](heads_of(h)), q_ref[h % 2]) * SCALE2
        for b in range(2):
            j = 2 * r + b
            block = (me ^ r) * 2 + b
            low, high = (bias_ref[head0 + h, (me * 2 + i) * NB + block] for i in range(2))
            z = s[b * 128 : (b + 1) * 128] + jnp.where(first_half, low, high)
            top = jnp.max(z.reshape(16, 8, ROWS), axis=0)
            tops[h] = top if tops[h] is None else jnp.maximum(tops[h], top)
            z_ref[h % 2, j * 128 : (j + 1) * 128] = z

    def power(h, r):
        if r == 0:
            tops[h] = jnp.max(tops[h], axis=0, keepdims=True)
        rows = slice(r * ROWS, (r + 1) * ROWS)
        p = jnp.exp2(z_ref[h % 2, rows] - tops[h])
        wt_ref[h, rows] = p.astype(BF16)
        part = jnp.sum(p.reshape(32, 8, ROWS), axis=0)
        sums[h] = part if sums[h] is None else sums[h] + part

    def finish(h):
        inv = 1.0 / jnp.sum(sums[h], axis=0, keepdims=True)
        inv_ref[h] = jnp.broadcast_to(inv, (8, ROWS))
        inv_rows = jnp.transpose(jnp.broadcast_to(inv, (R, ROWS)))
        scaled[h] = (g_ref[:, heads_of(h)].astype(F32) * inv_rows).astype(BF16)

    def low_grad(h, r):
        lgv_ref[r] += nn(wt_ref[h, r * ROWS : (r + 1) * ROWS], scaled[h])

    for i in range(GH + 2):
        if i < GH:
            prepare(i)
        for r in range(4):
            if i < GH:
                score(i, r)
            if 1 <= i <= GH:
                power(i - 1, r)
            if i >= 2:
                low_grad(i - 2, r)
        if 1 <= i <= GH:
            finish(i - 1)

    if last_call:

        @pl.when(step == pl.num_programs(0) - 1)
        def _():
            for i in range(2):
                here_ref[i] = lgv_ref[2 * i]
                sib_ref[i] = lgv_ref[2 * i + 1].astype(BF16)


def grad_kernel(
    first_call, downs,
    wt_ref, inv_ref, k0, k1, k2a, k2b, k3a, k3b, v0, v1, v2a, v2b, v3a, v3b, l0, l1, l2, l3,
    cot_ref, g_ref, upq_ref, upv_ref, lowqp_ref, perm_ref, *rest,
):
    core_ref, *rest = rest[0 if first_call else 1 :]
    if first_call:
        near_ref, far_ref, *rest = rest
    if downs:
        hidden_ref, here_ref, there_ref, low_query_ref, *rest = rest
    att_ref, lgq_ref, up_mine, up_other, *rest = rest
    if first_call:
        here_ref, there_ref, *rest = rest
    if downs:
        down_mine, down_other, *rest = rest
    vl_ref, back_ref, sh_ref, gu_ref, up_ref, *rest = rest
    step = pl.program_id(0)
    first_step, last_step = step == 0, step == pl.num_programs(0) - 1
    if downs:
        held_ref, sem = rest
        fetch = pltpu.make_async_copy(hidden_ref, held_ref, sem)
        pl.when(first_step)(fetch.start)
    keys = (
        lambda c: k0[:, c], lambda c: k1[:, c],
        functools.partial(of_step, k2a, k2b), functools.partial(of_step, k3a, k3b),
    )
    vals = (
        lambda c: v0[:, c], lambda c: v1[:, c],
        functools.partial(of_step, v2a, v2b), functools.partial(of_step, v3a, v3b),
    )
    lows = (l0, l1, l2, l3)

    @pl.when(first_step)
    def _():
        lgq_ref[...] = jnp.zeros_like(lgq_ref)
        if first_call:
            here_ref[...] = near_ref[0] + far_ref[0].astype(F32)
            there_ref[...] = (near_ref[1] + far_ref[1].astype(F32)).astype(BF16)
        for p in range(2):
            for r in range(4):
                vl_ref[p, r * ROWS : (r + 1) * ROWS, HD:] = lows[r][...]

    cot_g, dots, outs, dqs = [None] * GH, [None] * GH, [None] * GH, [None] * GH

    def prepare(h):
        c = heads_of(h)
        cot_g[h] = jnp.concatenate([cot_ref[:, c], g_ref[:, c]], axis=1)
        for r in range(4):
            vl_ref[h % 2, r * ROWS : (r + 1) * ROWS, :HD] = vals[r](c)

    def back(h, r):
        rows = slice(r * ROWS, (r + 1) * ROWS)
        b = nt(vl_ref[h % 2, rows], cot_g[h])
        back_ref[h % 2, rows] = b
        part = jnp.sum((b * wt_ref[h, rows].astype(F32)).reshape(32, 8, ROWS), axis=0)
        dots[h] = part if dots[h] is None else dots[h] + part

    def shift(h, r):
        rows = slice(r * ROWS, (r + 1) * ROWS)
        if r == 0:
            dots[h] = jnp.sum(dots[h], axis=0, keepdims=True) * inv_ref[h, 0:1]
        sh_ref[h % 2, rows] = (
            wt_ref[h, rows].astype(F32) * (back_ref[h % 2, rows] - dots[h])
        ).astype(BF16)
        if r == 3:
            key = jnp.concatenate([k(heads_of(h)) for k in keys], axis=0)
            dqs[h] = tn(key, sh_ref[h % 2])

    def attend(h):
        outs[h] = tn(vl_ref[h % 2], wt_ref[h])

    def finish_out(h):
        c = heads_of(h)
        out = outs[h] * inv_ref[h, 0:1]
        t1 = out[HD:].astype(BF16)
        att_ref[:, c] = (out[:HD] + tn(upv_ref[:, c], t1)).T.astype(BF16)
        t1_rows = nn(perm_ref[...], t1).astype(BF16)
        gu_ref[1, :, c] = nn(t1_rows, cot_ref[:, c])

    def finish_query(h):
        dq = (dqs[h] * (inv_ref[h, 0:1] * SCALE)).astype(BF16)
        gu_ref[0, :, heads_of(h)] = nt(lowqp_ref[...], dq)
        lgq_ref[...] += nn(upq_ref[:, heads_of(h)], dq)

    for i in range(GH + 2):
        if i < GH:
            prepare(i)
        for r in range(4):
            if i < GH:
                back(i, r)
            if 1 <= i <= GH:
                shift(i - 1, r)
        if i < GH:
            attend(i)
        if 1 <= i <= GH:
            finish_out(i - 1)
        if i >= 2:
            finish_query(i - 2)

    dp, count, _ = up_mine.shape
    for i in range(count):
        which, row, h = i // (count // 2), i // GH % (R // dp), i % GH
        up_ref[step, :, i, :] = gu_ref[which, row * dp : (row + 1) * dp, heads_of(h)]

    @pl.when(last_step)
    def _():
        first = core_ref[0, 0] == 0
        up_mine[...] = jnp.where(first, up_ref[0], up_ref[1]).astype(BF16)
        up_other[...] = jnp.where(first, up_ref[1], up_ref[0]).astype(BF16)
        if downs:
            query = low_query_ref[...] + lgq_ref[...]
            value = here_ref[...] + there_ref[...].astype(F32)
            low = jnp.concatenate([query.T, value], axis=1).astype(BF16)
            fetch.wait()
            down(core_ref, held_ref, low, down_mine, down_other)


def down(core_ref, hidden_ref, low, mine_ref, other_ref):
    first = core_ref[0, 0] == 0
    dests, rows, _ = mine_ref.shape
    rows //= 2
    group = min(8, dests)
    for g in range(dests // group):
        res = tn(hidden_ref[:, 2 * rows * group * g : 2 * rows * group * (g + 1)], low)
        for d in range(group):
            a0 = res[2 * d * rows : (2 * d + 1) * rows]
            a1 = res[(2 * d + 1) * rows : (2 * d + 2) * rows]
            for ref, a in ((mine_ref, jnp.where(first, a0, a1)), (other_ref, jnp.where(first, a1, a0))):
                ref[g * group + d] = jnp.concatenate([a[:, :R], a[:, R:]], axis=0).astype(BF16)


def col(off):
    return pl.BlockSpec((ROWS, GH * HD), lambda i: (0, i + off))


def group():
    return pl.BlockSpec((ROWS, GH * HD), lambda i: (0, 0))


def colup(off):
    return pl.BlockSpec((R, GH * HD), lambda i: (0, i + off))


def const(shape):
    return pl.BlockSpec(shape, lambda i: (0,) * len(shape))


def per_head(shape, off):
    return pl.BlockSpec((GH,) + shape, lambda i: (i + off,) + (0,) * len(shape))


def params():
    return pltpu.CompilerParams(dimension_semantics=("arbitrary",), vmem_limit_bytes=46 * 2**20)


def low_call(hidden, down_query, down_value):
    out = jax.ShapeDtypeStruct((ROWS, R), BF16)
    return pl.pallas_call(
        low_kernel,
        grid=(1,),
        in_specs=[const(hidden.shape), const(down_query.shape), const(down_value.shape)],
        out_specs=[const(out.shape)] * 2,
        out_shape=[out, out],
        compiler_params=params(),
        cost_estimate=pl.CostEstimate(flops=1_000_000, bytes_accessed=1_000, transcendentals=0),
        name="low_products",
    )(hidden, down_query, down_value)


def weight_call(c0, n, me, before, bias, query_base, lowq, upq, cot, upv, own, sib, zs, zd):
    keys = 4 * ROWS
    sums = jax.ShapeDtypeStruct((4, ROWS, R), F32)
    scratch = [pltpu.VMEM((2, keys, ROWS), F32), pltpu.VMEM((2, ROWS, HD), BF16)]
    if c0:
        extra, taken = [jax.ShapeDtypeStruct((2, ROWS, R), dtype) for dtype in (F32, BF16)], [before]
        scratch = [pltpu.VMEM(sums.shape, F32), *scratch]
    else:
        extra, taken = [sums], []
    return pl.pallas_call(
        functools.partial(weight_kernel, c0),
        grid=(n,),
        in_specs=[
            pl.BlockSpec(memory_space=pltpu.SMEM),
            pl.BlockSpec(memory_space=pltpu.SMEM),
            col(c0), const((ROWS, R)), colup(c0), col(c0), colup(c0),
            col(c0), col(c0), group(), group(), group(), group(),
            *[const(sums.shape) for _ in taken],
        ],
        out_specs=[
            per_head((keys, ROWS), 0), per_head((8, ROWS), 0), col(0), *[const(out.shape) for out in extra],
        ],
        out_shape=[
            jax.ShapeDtypeStruct((n * GH, keys, ROWS), BF16),
            jax.ShapeDtypeStruct((n * GH, 8, ROWS), F32),
            jax.ShapeDtypeStruct((ROWS, n * GH * HD), BF16),
            *extra,
        ],
        scratch_shapes=scratch,
        compiler_params=params(),
        cost_estimate=pl.CostEstimate(
            flops=1_000_000, bytes_accessed=1_000, transcendentals=0
        ),
        name="attention_weights",
    )(me.reshape(1, 1), bias, query_base, lowq, upq, cot, upv, own, sib, *zs, *zd, *taken)


def grad_call(c0, n, kc0, core, att, wt, inv, keys, vals, lows, cot, g, upq, upv, lowqp, perm, dp, low_sums, downs=None):
    off = c0 - kc0
    args = [wt, inv, *keys, *vals, *[low for low, _ in lows], cot, g, upq, upv, lowqp, perm]
    specs = [
        per_head((4 * ROWS, ROWS), off), per_head((8, ROWS), off),
        col(c0), col(c0), group(), group(), group(), group(),
        col(c0), col(c0), group(), group(), group(), group(),
        *[pl.BlockSpec((ROWS, R), functools.partial(lambda at, i: (0, at), at)) for _, at in lows],
        col(c0), col(off), colup(c0), colup(c0), const((R, ROWS)), const((R, R)),
    ]
    alias = {}
    if att is not None:
        alias = {len(args): 0}
        args.append(att)
        specs.append(pl.BlockSpec(memory_space=pl.ANY))
    args.append(core.reshape(1, 1))
    specs.append(pl.BlockSpec(memory_space=pltpu.SMEM))
    if not downs:
        args += low_sums
        specs += [const(low.shape) for low in low_sums]
    packed = (dp, 2 * (R // dp) * GH, HD)
    outs = [
        jax.ShapeDtypeStruct((ROWS, HEADS * HD), BF16),
        jax.ShapeDtypeStruct((R, ROWS), F32),
        jax.ShapeDtypeStruct(packed, BF16),
        jax.ShapeDtypeStruct(packed, BF16),
    ]
    if not downs:
        outs += [jax.ShapeDtypeStruct((ROWS, R), dtype) for dtype in (F32, BF16)]
    out_specs = [col(c0), *[const(out.shape) for out in outs[1:]]]
    scratch = [
        pltpu.VMEM((2, 4 * ROWS, HD + R), BF16),
        pltpu.VMEM((2, 4 * ROWS, ROWS), F32),
        pltpu.VMEM((2, 4 * ROWS, ROWS), BF16),
        pltpu.VMEM((2, R, GH * HD), F32),
        pltpu.VMEM((n,) + packed, F32),
    ]
    if downs:
        hidden, *lows = downs
        args += [hidden, *lows]
        specs += [pl.BlockSpec(memory_space=pl.ANY), *[const(low.shape) for low in lows]]
        halves = (2 * dp, hidden.shape[1] // (2 * dp), R)
        outs += [jax.ShapeDtypeStruct(halves, BF16)] * 2
        out_specs += [const(halves)] * 2
        scratch += [pltpu.VMEM(hidden.shape, BF16), pltpu.SemaphoreType.DMA]
    return pl.pallas_call(
        functools.partial(grad_kernel, att is None, bool(downs)),
        grid=(n,),
        in_specs=specs,
        out_specs=out_specs,
        out_shape=outs,
        scratch_shapes=scratch,
        input_output_aliases=alias,
        compiler_params=params(),
        cost_estimate=pl.CostEstimate(flops=1_000_000, bytes_accessed=1_000, transcendentals=0),
        name="attention_grads",
    )(*args)


DP = ("x", "zh", "y")
CORE_SWAP = [(0, 1), (1, 0)]


def over_core(a):
    return lax.ppermute(a, "core", CORE_SWAP)


def over_z(a):
    return lax.ppermute(a, "zl", CORE_SWAP)


def over_far_z(a):
    return lax.ppermute(a, ("zh", "zl"), [(0, 3), (1, 2), (2, 1), (3, 0)])


def per_device(
    hidden, query_base, key_base, value_base, cotangent,
    down_query, down_value, up_query, up_value, key_blocks, block_counts,
):
    dp = lax.axis_size(DP)
    core = lax.axis_index("core")
    me = lax.axis_index("zl") * 2 + core
    after = lax.optimization_barrier

    def columns(a, c0, n):
        return a[:, c0 * GH * HD : (c0 + n) * GH * HD]

    k_first = tuple(columns(key_base, g, 1) for g in (0, 1))
    key_rest, value_rest, k_first = after((key_base, value_base, k_first))
    k_zs = [tuple(over_z(a) for a in k_first)]
    k_sib = over_core(key_rest)
    k_sib, hidden, key_blocks, block_counts = after((k_sib, hidden, key_blocks, block_counts))

    listed = jnp.arange(key_blocks.shape[2])[None, None, :] < block_counts[:, :, None]
    allowed = jnp.any((key_blocks[..., None] == jnp.arange(NB)) & listed[..., None], axis=2)
    bias = jnp.where(allowed, 0.0, -1e30).astype(F32).reshape(GH, NB * NB)
    bias = jnp.stack([bias, over_far_z(bias)])
    bias = jnp.stack([bias, over_core(bias)], axis=1).reshape(HEADS, NB * NB)

    low_query, low_value = low_call(hidden, down_query, down_value)
    key_rest, low_query = after((key_rest, low_query))
    k_second = tuple(columns(key_rest, g, 1) for g in (2, 3))
    v_first = (jnp.concatenate([columns(value_rest, 0, 1), low_value], axis=1), columns(value_rest, 1, 1))
    v_second = tuple(columns(value_rest, g, 1) for g in (2, 3))
    low_query_p = low_query.T.reshape(dp, R // dp, ROWS).transpose(1, 0, 2).reshape(R, ROWS)
    turn = jnp.arange(R)
    turn = turn % dp * (R // dp) + turn // dp
    perm = (turn[:, None] == jnp.arange(R)[None, :]).astype(BF16)
    k_zs[0], low_query, low_query_p, perm, bias, k_second, v_second = after(
        (k_zs[0], low_query, low_query_p, perm, bias, k_second, v_second)
    )
    k_zs.append(tuple(over_z(a) for a in k_second))
    k_zd = [tuple(over_core(a) for a in k_zs[0])]
    v_zs = [tuple(over_z(a) for a in v_first)]
    v_sib = over_core(value_base)
    low_sib = over_core(low_value)

    weights, lgv = [], [None]
    for i, (c0, n) in enumerate(K_CHUNKS):
        if i:
            v_second, arrived, weights[-1] = after((v_second, k_zs[i], weights[-1]))
            k_zd.append(tuple(over_core(a) for a in arrived))
            v_zs.append(tuple(over_z(a) for a in v_second))
        wt, inv, g, *lgv = weight_call(
            c0, n, me, lgv[0], bias, query_base, low_query, up_query, cotangent, up_value,
            key_base, k_sib, k_zs[i], k_zd[i],
        )
        weights.append([wt, inv, g])
    near, far = lgv[0], over_core(lgv[1])

    def both(mine, other):
        return (mine.astype(F32) + over_core(other).astype(F32)).astype(BF16)

    att, v_zd = None, []
    for i, (c0, n) in enumerate(V_CHUNKS):
        which = [w for w, (a, m) in enumerate(K_CHUNKS) if a <= c0 < a + m][0]
        if i:
            arrived, att, lgv_there = after((v_zs[i], att, over_z(lgv_there)))
        else:
            arrived, weights[-1] = after((v_zs[i], weights[-1]))
        v_zd.append(tuple(over_core(a) for a in arrived))
        if not i:
            lows = [(low_value, 0), (low_sib, 0), (v_zs[0][0], GH), (v_zd[0][0], GH)]
        else:
            v_zd[i], up_first = after((v_zd[i], up_first))
        wt, inv, g = weights[which]
        att, *made = grad_call(
            c0, n, K_CHUNKS[which][0], core, att, wt, inv,
            (key_base, k_sib, *k_zs[which], *k_zd[which]), (value_base, v_sib, *v_zs[i], *v_zd[i]),
            lows, cotangent, g, up_query, up_value, low_query_p, perm, dp,
            (near, far), downs=(hidden, lgv_here, lgv_there, lgq) if i else None,
        )
        if not i:
            lgq, up_mine, up_other, lgv_here, lgv_there = made
            up_first = both(up_mine, up_other)
    up_mine, up_other, down_mine, down_other = made[1:]

    up = jnp.stack([up_first, both(up_mine, up_other)], axis=1)
    down_sum = both(down_mine, down_other)
    payload = jnp.concatenate([down_sum, up.reshape(2 * dp, -1, HD)], axis=1)
    landed = lax.all_to_all(payload, DP + ("zl",), 0, 0, tiled=True)
    total = jnp.sum(landed.astype(F32), axis=0)
    rows = hidden.shape[1] // (4 * dp)
    grad_down = total[: 2 * rows].reshape(2, rows, R).transpose(1, 0, 2)
    grad_up = total[2 * rows :].reshape(2, R // dp, GH * HD).transpose(1, 0, 2)
    return att, grad_down, grad_up


def solution(mesh):
    dp = mesh.devices.shape[0]
    side = math.isqrt(dp // 2)
    fine = Mesh(mesh.devices.reshape(side, 2, side, 2, 2), DP + ("zl", "core"))
    everyone = DP + ("zl", "core")
    tokens = P(everyone, None)
    return jax.shard_map(
        per_device,
        mesh=fine,
        in_specs=(
            tokens, tokens, tokens, tokens, tokens, P(), P(), P(), P(),
            P(("zl", "core"), None, None), P(("zl", "core"), None),
        ),
        out_specs=(tokens, P(everyone, None, None), P(DP, None, ("zl", "core"))),
        check_vma=False,
    )
```

```python
import functools
import math

import jax
import jax.numpy as jnp
from jax import lax
from jax.experimental import pallas as pl
from jax.experimental.pallas import tpu as pltpu
from jax.sharding import Mesh
from jax.sharding import PartitionSpec as P

HEADS = 20
HD = 128
R = 128
NB = 8
ROWS = 256
GH = 5
K_CHUNKS = ((0, 2), (2, 2))
V_CHUNKS = ((0, 2), (2, 2))
SCALE = 1.0 / math.sqrt(HD)
SCALE2 = SCALE * math.log2(math.e)
F32 = jnp.float32
BF16 = jnp.bfloat16


def nn(a, b):
    return lax.dot_general(a, b, (((1,), (0,)), ((), ())), preferred_element_type=F32)


def nt(a, b):
    return lax.dot_general(a, b, (((1,), (1,)), ((), ())), preferred_element_type=F32)


def tn(a, b):
    return lax.dot_general(a, b, (((0,), (0,)), ((), ())), preferred_element_type=F32)


def low_kernel(hidden_ref, down_query_ref, down_value_ref, query_ref, value_ref):
    query_ref[...] = nn(hidden_ref[...], down_query_ref[...]).astype(BF16)
    value_ref[...] = nn(hidden_ref[...], down_value_ref[...]).astype(BF16)


def heads_of(h):
    return slice(h * HD, (h + 1) * HD)


def of_step(a_ref, b_ref, cols):
    return jnp.where(pl.program_id(0) == 0, a_ref[:, cols], b_ref[:, cols])


def weight_kernel(
    chunk0, me_ref, bias_ref, qb_ref, lowq_ref, upq_ref, cot_ref, upv_ref, k0, k1, k2a, k2b, k3a, k3b, *rest
):
    step = pl.program_id(0)
    keys = (
        lambda c: k0[:, c], lambda c: k1[:, c],
        functools.partial(of_step, k2a, k2b), functools.partial(of_step, k3a, k3b),
    )
    last_call = chunk0 > 0
    if last_call:
        before_ref, *rest = rest
    wt_ref, inv_ref, g_ref, *rest = rest
    if last_call:
        here_ref, sib_ref, *rest = rest
    lgv_ref, z_ref, q_ref = rest
    first_half = lax.broadcasted_iota(jnp.int32, (1, ROWS), 1) < ROWS // 2
    me = me_ref[0, 0]
    head0 = ((chunk0 + step) ^ me) * GH

    @pl.when(step == 0)
    def _():
        lgv_ref[...] = before_ref[...] if last_call else jnp.zeros_like(lgv_ref)

    tops, sums, scaled = [None] * GH, [None] * GH, [None] * GH

    def prepare(h):
        c = heads_of(h)
        q_ref[h % 2] = (qb_ref[:, c].astype(F32) + nn(lowq_ref[...], upq_ref[:, c])).astype(BF16)
        g_ref[:, c] = nt(cot_ref[:, c], upv_ref[:, c]).astype(BF16)

    def score(h, r):
        s = nt(keys[r](heads_of(h)), q_ref[h % 2]) * SCALE2
        for b in range(2):
            j = 2 * r + b
            block = (me ^ r) * 2 + b
            low, high = (bias_ref[head0 + h, (me * 2 + i) * NB + block] for i in range(2))
            z = s[b * 128 : (b + 1) * 128] + jnp.where(first_half, low, high)
            top = jnp.max(z.reshape(16, 8, ROWS), axis=0)
            tops[h] = top if tops[h] is None else jnp.maximum(tops[h], top)
            z_ref[h % 2, j * 128 : (j + 1) * 128] = z

    def power(h, r):
        if r == 0:
            tops[h] = jnp.max(tops[h], axis=0, keepdims=True)
        rows = slice(r * ROWS, (r + 1) * ROWS)
        p = jnp.exp2(z_ref[h % 2, rows] - tops[h])
        wt_ref[h, rows] = p.astype(BF16)
        part = jnp.sum(p.reshape(32, 8, ROWS), axis=0)
        sums[h] = part if sums[h] is None else sums[h] + part

    def finish(h):
        inv = 1.0 / jnp.sum(sums[h], axis=0, keepdims=True)
        inv_ref[h] = jnp.broadcast_to(inv, (8, ROWS))
        inv_rows = jnp.transpose(jnp.broadcast_to(inv, (R, ROWS)))
        scaled[h] = (g_ref[:, heads_of(h)].astype(F32) * inv_rows).astype(BF16)

    def low_grad(h, r):
        lgv_ref[r] += nn(wt_ref[h, r * ROWS : (r + 1) * ROWS], scaled[h])

    for i in range(GH + 2):
        if i < GH:
            prepare(i)
        for r in range(4):
            if i < GH:
                score(i, r)
            if 1 <= i <= GH:
                power(i - 1, r)
            if i >= 2:
                low_grad(i - 2, r)
        if 1 <= i <= GH:
            finish(i - 1)

    if last_call:

        @pl.when(step == pl.num_programs(0) - 1)
        def _():
            for i in range(2):
                here_ref[i] = lgv_ref[2 * i]
                sib_ref[i] = lgv_ref[2 * i + 1].astype(BF16)


def grad_kernel(
    first_call, downs,
    wt_ref, inv_ref, k0, k1, k2a, k2b, k3a, k3b, v0, v1, v2a, v2b, v3a, v3b, l0, l1, l2, l3,
    cot_ref, g_ref, upq_ref, upv_ref, lowqp_ref, perm_ref, *rest,
):
    core_ref, *rest = rest[0 if first_call else 1 :]
    if first_call:
        near_ref, far_ref, *rest = rest
    if downs:
        hidden_ref, here_ref, there_ref, low_query_ref, *rest = rest
    att_ref, lgq_ref, up_mine, up_other, *rest = rest
    if first_call:
        here_ref, there_ref, *rest = rest
    if downs:
        down_mine, down_other, *rest = rest
    vl_ref, back_ref, sh_ref, gu_ref, up_ref, *rest = rest
    step = pl.program_id(0)
    first_step, last_step = step == 0, step == pl.num_programs(0) - 1
    if downs:
        held_ref, sem = rest
        fetch = pltpu.make_async_copy(hidden_ref, held_ref, sem)
        pl.when(first_step)(fetch.start)
    keys = (
        lambda c: k0[:, c], lambda c: k1[:, c],
        functools.partial(of_step, k2a, k2b), functools.partial(of_step, k3a, k3b),
    )
    vals = (
        lambda c: v0[:, c], lambda c: v1[:, c],
        functools.partial(of_step, v2a, v2b), functools.partial(of_step, v3a, v3b),
    )
    lows = (l0, l1, l2, l3)

    @pl.when(first_step)
    def _():
        lgq_ref[...] = jnp.zeros_like(lgq_ref)
        if first_call:
            here_ref[...] = near_ref[0] + far_ref[0].astype(F32)
            there_ref[...] = (near_ref[1] + far_ref[1].astype(F32)).astype(BF16)
        for p in range(2):
            for r in range(4):
                vl_ref[p, r * ROWS : (r + 1) * ROWS, HD:] = lows[r][...]

    cot_g, dots, outs, dqs = [None] * GH, [None] * GH, [None] * GH, [None] * GH

    def prepare(h):
        c = heads_of(h)
        cot_g[h] = jnp.concatenate([cot_ref[:, c], g_ref[:, c]], axis=1)
        for r in range(4):
            vl_ref[h % 2, r * ROWS : (r + 1) * ROWS, :HD] = vals[r](c)

    def back(h, r):
        rows = slice(r * ROWS, (r + 1) * ROWS)
        b = nt(vl_ref[h % 2, rows], cot_g[h])
        back_ref[h % 2, rows] = b
        part = jnp.sum((b * wt_ref[h, rows].astype(F32)).reshape(32, 8, ROWS), axis=0)
        dots[h] = part if dots[h] is None else dots[h] + part

    def shift(h, r):
        rows = slice(r * ROWS, (r + 1) * ROWS)
        if r == 0:
            dots[h] = jnp.sum(dots[h], axis=0, keepdims=True) * inv_ref[h, 0:1]
        sh_ref[h % 2, rows] = (
            wt_ref[h, rows].astype(F32) * (back_ref[h % 2, rows] - dots[h])
        ).astype(BF16)
        if r == 3:
            key = jnp.concatenate([k(heads_of(h)) for k in keys], axis=0)
            dqs[h] = tn(key, sh_ref[h % 2])

    def attend(h):
        outs[h] = tn(vl_ref[h % 2], wt_ref[h])

    def finish_out(h):
        c = heads_of(h)
        out = outs[h] * inv_ref[h, 0:1]
        t1 = out[HD:].astype(BF16)
        att_ref[:, c] = (out[:HD] + tn(upv_ref[:, c], t1)).T.astype(BF16)
        t1_rows = nn(perm_ref[...], t1).astype(BF16)
        gu_ref[1, :, c] = nn(t1_rows, cot_ref[:, c])

    def finish_query(h):
        dq = (dqs[h] * (inv_ref[h, 0:1] * SCALE)).astype(BF16)
        gu_ref[0, :, heads_of(h)] = nt(lowqp_ref[...], dq)
        lgq_ref[...] += nn(upq_ref[:, heads_of(h)], dq)

    for i in range(GH + 2):
        if i < GH:
            prepare(i)
        for r in range(4):
            if i < GH:
                back(i, r)
            if 1 <= i <= GH:
                shift(i - 1, r)
        if i < GH:
            attend(i)
        if 1 <= i <= GH:
            finish_out(i - 1)
        if i >= 2:
            finish_query(i - 2)

    dp, count, _ = up_mine.shape
    for i in range(count):
        which, row, h = i // (count // 2), i // GH % (R // dp), i % GH
        up_ref[step, :, i, :] = gu_ref[which, row * dp : (row + 1) * dp, heads_of(h)]

    @pl.when(last_step)
    def _():
        first = core_ref[0, 0] == 0
        up_mine[...] = jnp.where(first, up_ref[0], up_ref[1]).astype(BF16)
        up_other[...] = jnp.where(first, up_ref[1], up_ref[0]).astype(BF16)
        if downs:
            query = low_query_ref[...] + lgq_ref[...]
            value = here_ref[...] + there_ref[...].astype(F32)
            low = jnp.concatenate([query.T, value], axis=1).astype(BF16)
            fetch.wait()
            down(core_ref, held_ref, low, down_mine, down_other)


def down(core_ref, hidden_ref, low, mine_ref, other_ref):
    first = core_ref[0, 0] == 0
    dests, rows, _ = mine_ref.shape
    rows //= 2
    group = min(8, dests)
    for g in range(dests // group):
        res = tn(hidden_ref[:, 2 * rows * group * g : 2 * rows * group * (g + 1)], low)
        for d in range(group):
            a0 = res[2 * d * rows : (2 * d + 1) * rows]
            a1 = res[(2 * d + 1) * rows : (2 * d + 2) * rows]
            for ref, a in ((mine_ref, jnp.where(first, a0, a1)), (other_ref, jnp.where(first, a1, a0))):
                ref[g * group + d] = jnp.concatenate([a[:, :R], a[:, R:]], axis=0).astype(BF16)


def col(off):
    return pl.BlockSpec((ROWS, GH * HD), lambda i: (0, i + off))


def group():
    return pl.BlockSpec((ROWS, GH * HD), lambda i: (0, 0))


def colup(off):
    return pl.BlockSpec((R, GH * HD), lambda i: (0, i + off))


def const(shape):
    return pl.BlockSpec(shape, lambda i: (0,) * len(shape))


def per_head(shape, off):
    return pl.BlockSpec((GH,) + shape, lambda i: (i + off,) + (0,) * len(shape))


def params():
    return pltpu.CompilerParams(dimension_semantics=("arbitrary",), vmem_limit_bytes=46 * 2**20)


def low_call(hidden, down_query, down_value):
    out = jax.ShapeDtypeStruct((ROWS, R), BF16)
    return pl.pallas_call(
        low_kernel,
        grid=(1,),
        in_specs=[const(hidden.shape), const(down_query.shape), const(down_value.shape)],
        out_specs=[const(out.shape)] * 2,
        out_shape=[out, out],
        compiler_params=params(),
        cost_estimate=pl.CostEstimate(flops=1_000_000, bytes_accessed=1_000, transcendentals=0),
        name="low_products",
    )(hidden, down_query, down_value)


def weight_call(c0, n, me, before, bias, query_base, lowq, upq, cot, upv, own, sib, zs, zd):
    keys = 4 * ROWS
    sums = jax.ShapeDtypeStruct((4, ROWS, R), F32)
    scratch = [pltpu.VMEM((2, keys, ROWS), F32), pltpu.VMEM((2, ROWS, HD), BF16)]
    if c0:
        extra, taken = [jax.ShapeDtypeStruct((2, ROWS, R), dtype) for dtype in (F32, BF16)], [before]
        scratch = [pltpu.VMEM(sums.shape, F32), *scratch]
    else:
        extra, taken = [sums], []
    return pl.pallas_call(
        functools.partial(weight_kernel, c0),
        grid=(n,),
        in_specs=[
            pl.BlockSpec(memory_space=pltpu.SMEM),
            pl.BlockSpec(memory_space=pltpu.SMEM),
            col(c0), const((ROWS, R)), colup(c0), col(c0), colup(c0),
            col(c0), col(c0), group(), group(), group(), group(),
            *[const(sums.shape) for _ in taken],
        ],
        out_specs=[
            per_head((keys, ROWS), 0), per_head((8, ROWS), 0), col(0), *[const(out.shape) for out in extra],
        ],
        out_shape=[
            jax.ShapeDtypeStruct((n * GH, keys, ROWS), BF16),
            jax.ShapeDtypeStruct((n * GH, 8, ROWS), F32),
            jax.ShapeDtypeStruct((ROWS, n * GH * HD), BF16),
            *extra,
        ],
        scratch_shapes=scratch,
        compiler_params=params(),
        cost_estimate=pl.CostEstimate(
            flops=1_000_000, bytes_accessed=1_000, transcendentals=0
        ),
        name="attention_weights",
    )(me.reshape(1, 1), bias, query_base, lowq, upq, cot, upv, own, sib, *zs, *zd, *taken)


def grad_call(c0, n, kc0, core, att, wt, inv, keys, vals, lows, cot, g, upq, upv, lowqp, perm, dp, low_sums, downs=None):
    off = c0 - kc0
    args = [wt, inv, *keys, *vals, *[low for low, _ in lows], cot, g, upq, upv, lowqp, perm]
    specs = [
        per_head((4 * ROWS, ROWS), off), per_head((8, ROWS), off),
        col(c0), col(c0), group(), group(), group(), group(),
        col(c0), col(c0), group(), group(), group(), group(),
        *[pl.BlockSpec((ROWS, R), functools.partial(lambda at, i: (0, at), at)) for _, at in lows],
        col(c0), col(off), colup(c0), colup(c0), const((R, ROWS)), const((R, R)),
    ]
    alias = {}
    if att is not None:
        alias = {len(args): 0}
        args.append(att)
        specs.append(pl.BlockSpec(memory_space=pl.ANY))
    args.append(core.reshape(1, 1))
    specs.append(pl.BlockSpec(memory_space=pltpu.SMEM))
    if not downs:
        args += low_sums
        specs += [const(low.shape) for low in low_sums]
    packed = (dp, 2 * (R // dp) * GH, HD)
    outs = [
        jax.ShapeDtypeStruct((ROWS, HEADS * HD), BF16),
        jax.ShapeDtypeStruct((R, ROWS), F32),
        jax.ShapeDtypeStruct(packed, BF16),
        jax.ShapeDtypeStruct(packed, BF16),
    ]
    if not downs:
        outs += [jax.ShapeDtypeStruct((ROWS, R), dtype) for dtype in (F32, BF16)]
    out_specs = [col(c0), *[const(out.shape) for out in outs[1:]]]
    scratch = [
        pltpu.VMEM((2, 4 * ROWS, HD + R), BF16),
        pltpu.VMEM((2, 4 * ROWS, ROWS), F32),
        pltpu.VMEM((2, 4 * ROWS, ROWS), BF16),
        pltpu.VMEM((2, R, GH * HD), F32),
        pltpu.VMEM((n,) + packed, F32),
    ]
    if downs:
        hidden, *lows = downs
        args += [hidden, *lows]
        specs += [pl.BlockSpec(memory_space=pl.ANY), *[const(low.shape) for low in lows]]
        halves = (2 * dp, hidden.shape[1] // (2 * dp), R)
        outs += [jax.ShapeDtypeStruct(halves, BF16)] * 2
        out_specs += [const(halves)] * 2
        scratch += [pltpu.VMEM(hidden.shape, BF16), pltpu.SemaphoreType.DMA]
    return pl.pallas_call(
        functools.partial(grad_kernel, att is None, bool(downs)),
        grid=(n,),
        in_specs=specs,
        out_specs=out_specs,
        out_shape=outs,
        scratch_shapes=scratch,
        input_output_aliases=alias,
        compiler_params=params(),
        cost_estimate=pl.CostEstimate(flops=1_000_000, bytes_accessed=1_000, transcendentals=0),
        name="attention_grads",
    )(*args)


DP = ("x", "zh", "y")
CORE_SWAP = [(0, 1), (1, 0)]


def over_core(a):
    return lax.ppermute(a, "core", CORE_SWAP)


def over_z(a):
    return lax.ppermute(a, "zl", CORE_SWAP)


def over_far_z(a):
    return lax.ppermute(a, ("zh", "zl"), [(0, 3), (1, 2), (2, 1), (3, 0)])


def per_device(
    hidden, query_base, key_base, value_base, cotangent,
    down_query, down_value, up_query, up_value, key_blocks, block_counts,
):
    dp = lax.axis_size(DP)
    core = lax.axis_index("core")
    me = lax.axis_index("zl") * 2 + core
    after = lax.optimization_barrier

    def columns(a, c0, n):
        return a[:, c0 * GH * HD : (c0 + n) * GH * HD]

    k_first = tuple(columns(key_base, g, 1) for g in (0, 1))
    key_rest, value_rest, k_first = after((key_base, value_base, k_first))
    k_zs = [tuple(over_z(a) for a in k_first)]
    k_sib = over_core(key_rest)
    k_sib, hidden, key_blocks, block_counts = after((k_sib, hidden, key_blocks, block_counts))

    listed = jnp.arange(key_blocks.shape[2])[None, None, :] < block_counts[:, :, None]
    allowed = jnp.any((key_blocks[..., None] == jnp.arange(NB)) & listed[..., None], axis=2)
    bias = jnp.where(allowed, 0.0, -1e30).astype(F32).reshape(GH, NB * NB)
    bias = jnp.stack([bias, over_far_z(bias)])
    bias = jnp.stack([bias, over_core(bias)], axis=1).reshape(HEADS, NB * NB)

    low_query, low_value = low_call(hidden, down_query, down_value)
    key_rest, low_query = after((key_rest, low_query))
    k_second = tuple(columns(key_rest, g, 1) for g in (2, 3))
    v_first = (jnp.concatenate([columns(value_rest, 0, 1), low_value], axis=1), columns(value_rest, 1, 1))
    v_second = tuple(columns(value_rest, g, 1) for g in (2, 3))
    low_query_p = low_query.T.reshape(dp, R // dp, ROWS).transpose(1, 0, 2).reshape(R, ROWS)
    turn = jnp.arange(R)
    turn = turn % dp * (R // dp) + turn // dp
    perm = (turn[:, None] == jnp.arange(R)[None, :]).astype(BF16)
    low_sib = over_core(low_value)
    k_zs[0], low_query, low_query_p, perm, bias, k_second, v_second, low_sib = after(
        (k_zs[0], low_query, low_query_p, perm, bias, k_second, v_second, low_sib)
    )
    k_zs.append(tuple(over_z(a) for a in k_second))
    k_zd = [tuple(over_core(a) for a in k_zs[0])]
    v_zs = [tuple(over_z(a) for a in v_first)]
    v_sib = over_core(value_base)

    weights, lgv = [], [None]
    for i, (c0, n) in enumerate(K_CHUNKS):
        if i:
            v_second, arrived, weights[-1] = after((v_second, k_zs[i], weights[-1]))
            k_zd.append(tuple(over_core(a) for a in arrived))
            v_zs.append(tuple(over_z(a) for a in v_second))
        wt, inv, g, *lgv = weight_call(
            c0, n, me, lgv[0], bias, query_base, low_query, up_query, cotangent, up_value,
            key_base, k_sib, k_zs[i], k_zd[i],
        )
        weights.append([wt, inv, g])
    near, far = lgv[0], over_core(lgv[1])

    def both(mine, other):
        return (mine.astype(F32) + over_core(other).astype(F32)).astype(BF16)

    att, v_zd = None, []
    for i, (c0, n) in enumerate(V_CHUNKS):
        which = [w for w, (a, m) in enumerate(K_CHUNKS) if a <= c0 < a + m][0]
        if i:
            arrived, att, lgv_there = after((v_zs[i], att, over_z(lgv_there)))
        else:
            arrived, weights[-1] = after((v_zs[i], weights[-1]))
        v_zd.append(tuple(over_core(a) for a in arrived))
        if not i:
            lows = [(low_value, 0), (low_sib, 0), (v_zs[0][0], GH), (v_zd[0][0], GH)]
        else:
            v_zd[i], up_first = after((v_zd[i], up_first))
        wt, inv, g = weights[which]
        att, *made = grad_call(
            c0, n, K_CHUNKS[which][0], core, att, wt, inv,
            (key_base, k_sib, *k_zs[which], *k_zd[which]), (value_base, v_sib, *v_zs[i], *v_zd[i]),
            lows, cotangent, g, up_query, up_value, low_query_p, perm, dp,
            (near, far), downs=(hidden, lgv_here, lgv_there, lgq) if i else None,
        )
        if not i:
            lgq, up_mine, up_other, lgv_here, lgv_there = made
            up_first = both(up_mine, up_other)
    up_mine, up_other, down_mine, down_other = made[1:]

    up = jnp.stack([up_first, both(up_mine, up_other)], axis=1)
    down_sum = both(down_mine, down_other)
    payload = jnp.concatenate([down_sum, up.reshape(2 * dp, -1, HD)], axis=1)
    landed = lax.all_to_all(payload, DP + ("zl",), 0, 0, tiled=True)
    total = jnp.sum(landed.astype(F32), axis=0)
    rows = hidden.shape[1] // (4 * dp)
    grad_down = total[: 2 * rows].reshape(2, rows, R).transpose(1, 0, 2)
    grad_up = total[2 * rows :].reshape(2, R // dp, GH * HD).transpose(1, 0, 2)
    return att, grad_down, grad_up


def solution(mesh):
    dp = mesh.devices.shape[0]
    side = math.isqrt(dp // 2)
    fine = Mesh(mesh.devices.reshape(side, 2, side, 2, 2), DP + ("zl", "core"))
    everyone = DP + ("zl", "core")
    tokens = P(everyone, None)
    return jax.shard_map(
        per_device,
        mesh=fine,
        in_specs=(
            tokens, tokens, tokens, tokens, tokens, P(), P(), P(), P(),
            P(("zl", "core"), None, None), P(("zl", "core"), None),
        ),
        out_specs=(tokens, P(everyone, None, None), P(DP, None, ("zl", "core"))),
        check_vma=False,
    )
```
